32 devices in a mesh: tm: 4 (over y, x), space: 8 (over z, core).
Axes of the slice: x: 2, y: 2, z: 4, core: 2. Of those that a mesh axis runs over, the one named last changes fastest.
Arguments:
- video: bfloat16 [16, 16, 24, 3072], P('tm', 'space'), may hold values from -6 to 6
- w_qkv: bfloat16 [3072, 8, 384], P(None, 'space'), may hold values from -0.109375 to 0.109375
- w_out: bfloat16 [8, 128, 3072], P('space'), may hold values from -0.5 to 0.5
- q_gain: float32 [128], replicated, may hold values from 1 to 8
- k_gain: float32 [128], replicated, may hold values from 1 to 8
- tile_perm: int32 [4, 1536], P('tm'), may hold values from 0 to 1535, as said below
- window: int32 [6, 6], replicated, may hold values from 0 to 5, as said below
Outputs:
- mixed: bfloat16 [4, 1536, 3072], P('tm', 'space')
The draws below stay inside these ranges and needn't reach their ends.
Inputs may be any that keep to these rules, and one draw needn't show every extreme that they name: `tile_perm`: each row is a permutation of the slots of one frame group in which slots t*256 to t*256 + 255 hold exactly the tokens of tile t; tile t covers frames of the group, rows (t // 3) * 8 onward and columns (t % 3) * 8 onward, 8 and 8 of them. `window`: row t holds 6 different tiles, the first being t.
All inputs are finite; a program needn't handle non-finite values.
Results may differ from the reference program's by a relative error of at most 0.023.
The reference program's roundings to bfloat16 on the way count: a program that leaves them out, or rounds other values in their place, can miss the bound.
Values may be sent and summed in bfloat16 or wider, within the bound.
A program may use at most 128 MiB of HBM per device.

```python
import jax
import jax.numpy as jnp
from jax import lax

D = 3072
HD = 128
HEAD_DEV = 1
HEADS = 8
TH = 8
TW = 8
WIN = 6
W = 24
ROWS = 16
GROUPS = 4
FRAMES = 16
TILE = 256
NTS = 6
GTOK = 1536
N_SPACE = 8


def gain_values(key):
    return jnp.exp(jax.random.uniform(key, (HD,), jnp.float32, 0.0, 1.0986))


def draw_q_gain(key, part):
    key = jax.random.fold_in(key, 13)
    return gain_values(key)


def draw_k_gain(key, part):
    key = jax.random.fold_in(key, 14)
    return gain_values(key)


def draw_tile_perm(key, part):
    key = jax.random.fold_in(key, 11)
    tile_cols = W // TW
    slot = jnp.arange(GTOK, dtype=jnp.int32)
    tile_index = slot // TILE
    inner = slot % TILE
    tile_row = tile_index // tile_cols
    tile_col = tile_index % tile_cols
    frame = inner // (TH * TW)
    row_in = inner // TW % TH
    col_in = inner % TW
    raster = frame * ROWS * W + (tile_row * TH + row_in) * W + tile_col * TW + col_in
    base = raster.reshape(NTS, TILE)
    scores = jax.random.randint(key, (GROUPS, NTS, TILE), 0, 1 << 20, jnp.int32) * TILE
    scores = scores + jnp.arange(TILE, dtype=jnp.int32)[None, None, :]
    order = jnp.argsort(scores, axis=-1).astype(jnp.int32)
    shuffled = jnp.take_along_axis(jnp.broadcast_to(base[None], (GROUPS, NTS, TILE)), order, axis=-1)
    return shuffled.reshape(GROUPS, GTOK).astype(jnp.int32)


def draw_window(key, part):
    key = jax.random.fold_in(key, 12)
    scores = jax.random.randint(key, (NTS, NTS), 0, 1 << 20, jnp.int32) * NTS
    scores = scores + jnp.arange(NTS, dtype=jnp.int32)[None, :]
    scores = jnp.where(jnp.eye(NTS, dtype=jnp.bool_), -1, scores)
    return jnp.argsort(scores, axis=1)[:, :WIN].astype(jnp.int32)


def block_scale(own_key, extent, shards, least, top_value):
    def one(axis_at, blocks):
        steps = jax.random.uniform(jax.random.fold_in(jax.random.fold_in(own_key, 6), axis_at), (blocks,), jnp.float32, least / len(shards), top_value / len(shards))
        return jnp.repeat(jnp.exp(steps), extent[axis_at] // blocks).reshape((-1,) + (1,) * (len(extent) - axis_at - 1))

    loudness = one(*shards[0])
    for cut in shards[1:]:
        loudness = loudness * one(*cut)
    return loudness


def normal_values(key, extent, scale, most, pieces=(), kind=jnp.bfloat16):
    factor_of = block_scale(key, extent, pieces, -0.22, 0.18) if pieces else 1.0
    values = jax.random.normal(key, extent, jnp.float32) * scale * factor_of
    return jnp.minimum(jnp.maximum(values, -most), most).astype(kind)


def setup_inputs(seed: int = 0) -> dict:
    streams_of = jax.random.split(jax.random.key(seed), 8)
    video = normal_values(streams_of[0], (FRAMES, ROWS, W, D), 1.0, 6.0, ((0, 4), (1, 8)))
    w_qkv = normal_values(streams_of[1], (D, HEADS, 3 * HD), D ** -0.5, 0.109375, ((1, 8),))
    w_out = normal_values(streams_of[2], (HEADS, HD, D), HD ** -0.5, 0.5, ((0, 8),))
    q_gain = draw_q_gain(jax.random.fold_in(streams_of[7], 71), 0)
    k_gain = draw_k_gain(jax.random.fold_in(streams_of[7], 71), 0)
    tile_perm = draw_tile_perm(jax.random.fold_in(streams_of[7], 71), 0)
    window = draw_window(jax.random.fold_in(streams_of[7], 71), 0)
    return dict(video=video, w_qkv=w_qkv, w_out=w_out, q_gain=q_gain, k_gain=k_gain, tile_perm=tile_perm, window=window)


def head_norm(values, gain):
    wide = values.astype(jnp.float32)
    scaled = wide * lax.rsqrt(lax.optimization_barrier(jnp.mean(wide * wide, axis=-1, keepdims=True)) + 1e-06)
    return (scaled * gain).astype(jnp.bfloat16)

def attend(queries, chosen, valid):
    heads_here = queries.shape[1]
    head_dim = queries.shape[2]
    span = chosen.shape[1] * chosen.shape[2]
    keys = chosen[:, :, :, :, 0, :].reshape(-1, heads_here, head_dim)
    values = chosen[:, :, :, :, 1, :].reshape(-1, heads_here, head_dim)
    scores = jnp.einsum('qhd,khd->hqk', queries.astype(jnp.float32), keys.astype(jnp.float32)) * head_dim ** (-0.5)
    live = jnp.repeat(valid, span)
    scores = jnp.where(live[None, None, :], scores, -jnp.inf)
    highest = lax.optimization_barrier(jnp.max(scores, axis=-1, keepdims=True))
    weights = jnp.exp(scores - highest)
    probs = (weights / lax.optimization_barrier(jnp.sum(weights, axis=-1, keepdims=True))).astype(jnp.bfloat16)
    result = jnp.einsum('hqk,khd->qhd', probs.astype(jnp.float32), values.astype(jnp.float32))
    return result.astype(jnp.bfloat16)

def reference(video, w_qkv, w_out, q_gain, k_gain, tile_perm, window):
    flat_w = w_qkv.reshape(D, HEADS * 3 * HD)
    tokens = video.reshape(GROUPS, GTOK, D)

    def project(pair):
        group_tokens, order = pair
        qkv = jnp.dot(group_tokens, flat_w, preferred_element_type=jnp.float32).astype(jnp.bfloat16)
        qkv = qkv.reshape(GTOK, HEADS, 3, HD)
        ordered = jnp.take(qkv, order, axis=0)
        queries = head_norm(ordered[:, :, 0, :], q_gain)
        keys = head_norm(ordered[:, :, 1, :], k_gain)
        return (queries, jnp.stack([keys, ordered[:, :, 2, :]], axis=2))
    query_all, pairs_all = lax.map(project, (tokens, tile_perm))
    pairs_all = pairs_all.reshape(GROUPS, NTS, TILE, HEADS, 2, HD)
    blank = jnp.zeros((1,) + pairs_all.shape[1:], jnp.bfloat16)
    padded = jnp.concatenate([blank, pairs_all, blank], axis=0)

    def group_out(group_index):
        near = lax.dynamic_slice_in_dim(padded, group_index, 3, 0)
        valid = jnp.stack([group_index > 0, group_index >= 0, group_index < GROUPS - 1])
        query_group = lax.dynamic_index_in_dim(query_all, group_index, 0, keepdims=False)
        query_tiles = query_group.reshape(NTS, TILE, HEADS, HD)

        def one_tile(item):
            block, picks = item
            return attend(block, jnp.take(near, picks, axis=1), valid)
        return lax.map(one_tile, (query_tiles, window)).reshape(GTOK, HEADS * HD)
    attn_all = lax.map(group_out, jnp.arange(GROUPS, dtype=jnp.int32))
    flat_attn = attn_all.reshape(GROUPS * GTOK, N_SPACE, HEAD_DEV * HD)
    out_w = w_out.reshape(N_SPACE, HEAD_DEV * HD, D)

    def add_group(total, index):
        part_in = lax.dynamic_index_in_dim(flat_attn, index, 1, keepdims=False)
        part_w = lax.dynamic_index_in_dim(out_w, index, 0, keepdims=False)
        term = jnp.dot(part_in, part_w, preferred_element_type=jnp.float32)
        rounded = lax.optimization_barrier(term.astype(jnp.bfloat16)).astype(jnp.float32)
        return (total + rounded, None)
    start_total = jnp.zeros((GROUPS * GTOK, D), jnp.float32)
    total, unused = lax.scan(add_group, start_total, jnp.arange(N_SPACE, dtype=jnp.int32))
    return total.astype(jnp.bfloat16).reshape(GROUPS, GTOK, D)
```

```python
import functools
import math

import jax
import jax.numpy as jnp
from jax import lax
from jax.experimental import pallas as pl
from jax.experimental.pallas import tpu as pltpu
from jax.sharding import PartitionSpec as P

MESH = pl.DeviceIdType.MESH
TT = 4
TH = 8
TW = 8


def fused_kernel(
    n_tm,
    n_z,
    x_ref,
    wq_ref,
    wo_ref,
    qg_ref,
    kg_ref,
    pos_ref,
    out_ref,
    xg,
    wall,
    queries,
    kv,
    scores,
    attn,
    attn_in,
    part_out,
    part_in,
    wz_send,
    wz_recv,
    wt_send,
    wt_recv,
    x_send,
    x_recv,
    sib_send,
    sib_recv,
    kv_send,
    kv_recv,
    at_send,
    at_recv,
    pt_send,
    pt_recv,
):
    tm = lax.axis_index("tm")
    space = lax.axis_index("space")
    z = space // 2
    core = space % 2
    sibling = z * 2 + 1 - core
    tokens, model = x_ref.shape
    shards = 2 * n_z
    group = shards * tokens
    hd = kv.shape[2] // 3
    quarter = model // n_tm

    def remote(src, dst, send, recv, t, s):
        return pltpu.make_async_remote_copy(
            src_ref=src, dst_ref=dst, send_sem=send, recv_sem=recv,
            device_id=(t, s), device_id_type=MESH,
        )

    def rows_of(index, count):
        return pl.ds(pl.multiple_of(index * count, count), count)

    def w_ring(way, u, zz):
        target = z + 1 if way == 0 else z - 1
        block = wall.at[tm, rows_of(zz, hd)]
        return remote(block, block, wz_send.at[way, u], wz_recv.at[way, u], tm, target * 2 + core)

    def x_ring(way, u, zz):
        target = z + 1 if way == 0 else z - 1
        block = xg.at[zz * 2 + core]
        return remote(block, block, x_send.at[way, u], x_recv.at[way, u], tm, target * 2 + core)

    def w_peer(k, zz, owner):
        block = wall.at[owner, rows_of(zz, hd)]
        return remote(
            block, block, wt_send.at[k - 1, zz], wt_recv.at[k - 1, zz], (tm + k) % n_tm, space
        )

    def x_sibling(zz, side):
        block = xg.at[zz * 2 + side]
        return remote(block, block, sib_send.at[zz], sib_recv.at[zz], tm, sibling)

    def kv_copy(way, slot):
        target = tm - 1 if way == 0 else tm + 1
        rows = rows_of(slot, tokens)
        return remote(
            kv.at[0, rows, pl.ds(0, 2 * hd)],
            kv.at[2 - way, rows, pl.ds(0, 2 * hd)],
            kv_send.at[way, slot],
            kv_recv.at[way, slot],
            target,
            space,
        )

    def attn_copy(zz):
        return remote(
            attn.at[zz], attn_in.at[z], at_send.at[zz], at_recv.at[z], tm, zz * 2 + core
        )

    def attn_arrival(zz):
        return remote(
            attn.at[zz], attn_in.at[zz], at_send.at[zz], at_recv.at[zz], tm, zz * 2 + core
        )

    def part_copy(j):
        return remote(
            part_out.at[j], part_in.at[j], pt_send.at[j], pt_recv.at[j], tm, sibling
        )

    barrier = pltpu.get_barrier_semaphore()
    for k in range(1, n_z):
        pl.semaphore_signal(
            barrier, inc=1, device_id=(tm, (z + k) % n_z * 2 + core), device_id_type=MESH
        )
    for k in range(1, n_tm):
        pl.semaphore_signal(barrier, inc=1, device_id=((tm + k) % n_tm, space), device_id_type=MESH)
    pl.semaphore_signal(barrier, inc=1, device_id=(tm, sibling), device_id_type=MESH)
    for j in range(n_tm):
        wall[j, rows_of(z, hd), :] = wo_ref[:, j * quarter : (j + 1) * quarter]
    xg[space] = x_ref[...]
    kv[0, :, 2 * hd :] = jnp.ones((group, hd), jnp.bfloat16)
    pl.semaphore_wait(barrier, n_z - 1 + n_tm - 1 + 1)

    def norm(value, gain):
        scaled = value * lax.rsqrt(jnp.mean(value * value, axis=-1, keepdims=True) + 1e-06)
        return (scaled * gain).astype(jnp.bfloat16)

    def project(slot):
        rows = rows_of(slot, tokens)
        qkv = jnp.dot(xg[slot], wq_ref[...], preferred_element_type=jnp.float32)
        qkv = qkv.astype(jnp.bfloat16)
        queries[rows, :] = norm(qkv[:, :hd].astype(jnp.float32), qg_ref[...])
        kv[0, rows, 0:hd] = norm(qkv[:, hd : 2 * hd].astype(jnp.float32), kg_ref[...])
        kv[0, rows, hd : 2 * hd] = qkv[:, 2 * hd :]

    def inside(zz):
        return jnp.logical_and(zz >= 0, zz < n_z)

    def forwards(way):
        return z < n_z - 1 if way == 0 else z > 0

    def step(u, carry):
        for way in (0, 1):
            zz = z - u if way == 0 else z + u
            live = inside(zz)

            @pl.when(jnp.logical_and(live, u > 0))
            def _():
                w_ring(way, u - 1, zz).wait_recv()

            @pl.when(jnp.logical_and(live, forwards(way)))
            def _():
                w_ring(way, u, zz).start()

            @pl.when(jnp.logical_and(live, u > 0))
            def _():
                for k in range(1, n_tm):
                    w_peer(k, zz, tm).start()

        for way in (0, 1):
            zz = z - u if way == 0 else z + u
            live = inside(zz)
            fresh = live if way == 0 else jnp.logical_and(live, u > 0)

            @pl.when(jnp.logical_and(live, u > 0))
            def _():
                x_ring(way, u - 1, zz).wait_recv()

            @pl.when(jnp.logical_and(live, forwards(way)))
            def _():
                x_ring(way, u, zz).start()

            @pl.when(fresh)
            def _():
                x_sibling(zz, core).start()

        def item(i, carry):
            way = i % 2
            other = i // 2
            zz = z - u + way * 2 * u
            fresh = jnp.logical_and(inside(zz), way * (1 - jnp.minimum(u, 1)) == 0)

            @pl.when(fresh)
            def _():
                @pl.when(other == 1)
                def _():
                    x_sibling(zz, 1 - core).wait_recv()

                slot = zz * 2 + core + other * (1 - 2 * core)
                project(slot)

                @pl.when(tm > 0)
                def _():
                    kv_copy(0, slot).start()

                @pl.when(tm < n_tm - 1)
                def _():
                    kv_copy(1, slot).start()

            return carry

        lax.fori_loop(0, 4, item, 0)
        return carry

    lax.fori_loop(0, n_z, step, 0)

    for way in (0, 1):
        here = 2 - way
        live = tm < n_tm - 1 if way == 0 else tm > 0

        @pl.when(live)
        def _():
            kv[here, :, 2 * hd :] = jnp.ones((group, hd), jnp.bfloat16)

            def arrive(slot, carry):
                kv_copy(way, slot).wait_recv()
                return carry

            lax.fori_loop(0, shards, arrive, 0)

        @pl.when(jnp.logical_not(live))
        def _():
            kv[here, :, 0:hd] = kv[0, :, 0:hd]
            kv[here, :, hd:] = jnp.zeros((group, 2 * hd), jnp.bfloat16)

    factor = math.log2(math.e) * hd**-0.5
    block_rows = 2 * tokens

    def attend_block(i, carry):
        zz = (z + 1 + i) % n_z
        pos = pos_ref[rows_of(zz, block_rows), :]
        lanes = lax.broadcasted_iota(jnp.int32, (block_rows, group), 1)
        pick = jnp.where(lanes == pos, 1.0, 0.0).astype(jnp.bfloat16)
        query = jnp.dot(pick, queries[...], preferred_element_type=jnp.float32)
        query = query.astype(jnp.bfloat16)
        highest = None
        for part in range(3):
            score = lax.dot_general(
                query,
                kv[part, :, 0:hd],
                (((1,), (1,)), ((), ())),
                preferred_element_type=jnp.float32,
            )
            scores[part] = score
            top = jnp.max(score, axis=-1, keepdims=True)
            highest = top if highest is None else jnp.maximum(highest, top)
        total = jnp.zeros((block_rows, 2 * hd), jnp.float32)
        for part in range(3):
            weights = jnp.exp2((scores[part] - highest) * factor).astype(jnp.bfloat16)
            total += jnp.dot(weights, kv[part, :, hd:], preferred_element_type=jnp.float32)
        result = (total[:, :hd] / total[:, hd:]).astype(jnp.bfloat16)

        @pl.when(zz == z)
        def _():
            attn_in[z] = result

        @pl.when(zz != z)
        def _():
            attn[zz] = result
            attn_copy(zz).start()

        return carry

    lax.fori_loop(0, n_z, attend_block, 0)

    def others(body):
        for k in range(1, n_z):
            body((z + k) % n_z)

    def weights_in(zz):
        for k in range(1, n_tm):
            w_peer(k, zz, (tm + n_tm - k) % n_tm).wait_recv()

    others(weights_in)
    others(lambda zz: attn_arrival(zz).wait_recv())

    def mixed(side, j):
        rows = rows_of(side, tokens)
        left = jnp.concatenate([attn_in[zz, rows, :] for zz in range(n_z)], axis=1)
        return jnp.dot(left, wall[j], preferred_element_type=jnp.float32)

    for j in range(n_tm):
        part_out[j] = mixed(1 - core, j).astype(jnp.bfloat16)
        part_copy(j).start()
    for j in range(n_tm):
        own = mixed(core, j)
        part_copy(j).wait_recv()
        total = own + part_in[j].astype(jnp.float32)
        out_ref[:, j * quarter : (j + 1) * quarter] = total.astype(jnp.bfloat16)

    for j in range(n_tm):
        part_copy(j).wait_send()

    def sent(zz):
        attn_copy(zz).wait_send()
        for k in range(1, n_tm):
            w_peer(k, zz, tm).wait_send()

    others(sent)

    def drain(slot, carry):
        @pl.when(tm > 0)
        def _():
            kv_copy(0, slot).wait_send()

        @pl.when(tm < n_tm - 1)
        def _():
            kv_copy(1, slot).wait_send()

        return carry

    lax.fori_loop(0, shards, drain, 0)
    for zz in range(n_z):
        x_sibling(zz, core).wait_send()
    for u in range(n_z - 1):
        for way in (0, 1):
            zz = z - u if way == 0 else z + u

            @pl.when(jnp.logical_and(inside(zz), forwards(way)))
            def _():
                w_ring(way, u, zz).wait_send()
                x_ring(way, u, zz).wait_send()


def fused(n_tm, n_z, x, wq, wo, q_gain, k_gain, pos):
    tokens, model = x.shape
    hd = wo.shape[0]
    shards = 2 * n_z
    group = shards * tokens
    bf = jnp.bfloat16
    dma = pltpu.SemaphoreType.DMA
    vmem = pl.BlockSpec(memory_space=pltpu.VMEM)
    return pl.pallas_call(
        functools.partial(fused_kernel, n_tm, n_z),
        out_shape=jax.ShapeDtypeStruct((tokens, model), bf),
        in_specs=[vmem] * 6,
        out_specs=vmem,
        scratch_shapes=[
            pltpu.VMEM((shards, tokens, model), bf),
            pltpu.VMEM((n_tm, n_z * hd, model // n_tm), bf),
            pltpu.VMEM((group, hd), bf),
            pltpu.VMEM((3, group, 3 * hd), bf),
            pltpu.VMEM((3, 2 * tokens, group), jnp.float32),
            pltpu.VMEM((n_z, 2 * tokens, hd), bf),
            pltpu.VMEM((n_z, 2 * tokens, hd), bf),
            pltpu.VMEM((n_tm, tokens, model // n_tm), bf),
            pltpu.VMEM((n_tm, tokens, model // n_tm), bf),
            dma((2, n_z)),
            dma((2, n_z)),
            dma((n_tm - 1, n_z)),
            dma((n_tm - 1, n_z)),
            dma((2, n_z)),
            dma((2, n_z)),
            dma((n_z,)),
            dma((n_z,)),
            dma((2, shards)),
            dma((2, shards)),
            dma((n_z,)),
            dma((n_z,)),
            dma((n_tm,)),
            dma((n_tm,)),
        ],
        compiler_params=pltpu.CompilerParams(
            collective_id=0, has_side_effects=True, vmem_limit_bytes=56 * 1024 * 1024
        ),
    )(x, wq, wo, q_gain, k_gain, pos)


def whole_window(video, w_qkv, w_out, q_gain, k_gain, tile_perm):
    frames, rows_here, cols, model = video.shape
    n_tm = lax.axis_size("tm")
    n_space = lax.axis_size("space")
    hd = w_out.shape[1]
    place = tile_perm[0]
    rows = rows_here * n_space
    frame = place // (rows * cols)
    row = place // cols % rows
    col = place % cols
    tokens = frames * rows_here * cols
    pos = (row // rows_here) * tokens + (frame * rows_here + row % rows_here) * cols + col
    mixed = fused(
        n_tm,
        n_space // 2,
        video.reshape(tokens, model),
        w_qkv.reshape(model, 3 * hd),
        w_out.reshape(hd, model),
        q_gain.reshape(1, hd),
        k_gain.reshape(1, hd),
        pos.reshape(-1, 1),
    )
    return mixed[None]


def extended(cells, sides, width):
    for axis, dim in sides:
        count = lax.axis_size(axis)
        ends = count - 1
        head = lax.slice_in_dim(cells, 0, width, axis=dim)
        tail = lax.slice_in_dim(cells, cells.shape[dim] - width, cells.shape[dim], axis=dim)
        cells = jnp.concatenate(
            [
                lax.ppermute(tail, axis, [(i, (i + 1) % count) for i in range(ends)]),
                cells,
                lax.ppermute(head, axis, [((i + 1) % count, i) for i in range(ends)]),
            ],
            axis=dim,
        )
    return cells


def head_norm(values, gain):
    wide = values.astype(jnp.float32)
    scaled = wide * lax.rsqrt(jnp.mean(wide * wide, axis=-1, keepdims=True) + 1e-06)
    return (scaled * gain).astype(jnp.bfloat16)


def attend(queries, chosen, valid):
    heads_here = queries.shape[1]
    head_dim = queries.shape[2]
    span = chosen.shape[1] * chosen.shape[2]
    keys = chosen[:, :, :, :, 0, :].reshape(-1, heads_here, head_dim)
    values = chosen[:, :, :, :, 1, :].reshape(-1, heads_here, head_dim)
    scores = jnp.einsum(
        "qhd,khd->hqk", queries, keys, preferred_element_type=jnp.float32
    ) * head_dim ** (-0.5)
    live = jnp.repeat(valid, span)
    scores = jnp.where(live[None, None, :], scores, -jnp.inf)
    highest = jnp.max(scores, axis=-1, keepdims=True)
    weights = jnp.exp(scores - highest)
    probs = (weights / jnp.sum(weights, axis=-1, keepdims=True)).astype(jnp.bfloat16)
    result = jnp.einsum("hqk,khd->qhd", probs, values, preferred_element_type=jnp.float32)
    return result.astype(jnp.bfloat16)


def per_device(video, w_qkv, w_out, q_gain, k_gain, tile_perm, window):
    tiles = video.shape[0] * video.shape[1] * lax.axis_size("space") * video.shape[2] // (TT * TH * TW)
    if window.shape[1] == tiles and w_qkv.shape[1] == 1:
        return whole_window(video, w_qkv, w_out, q_gain, k_gain, tile_perm)
    frames_here = video.shape[0]
    cols_here = video.shape[2]
    model_dim = video.shape[3]
    heads_here = w_qkv.shape[1]
    head_dim = w_out.shape[1]
    flat_w = w_qkv.reshape(model_dim, heads_here * 3 * head_dim)
    qkv = jnp.einsum(
        "frwd,dc->frwc",
        lax.all_gather(video, "space", axis=1, tiled=True),
        flat_w,
        preferred_element_type=jnp.float32,
    ).astype(jnp.bfloat16)
    group_tokens = frames_here * qkv.shape[1] * cols_here
    qkv = qkv.reshape(group_tokens, heads_here, 3, head_dim)
    ordered = jnp.take(qkv, tile_perm[0], axis=0)
    queries = head_norm(ordered[:, :, 0, :], q_gain)
    keys = head_norm(ordered[:, :, 1, :], k_gain)
    pairs = jnp.stack([keys, ordered[:, :, 2, :]], axis=2)
    beside_all = extended(pairs[None], (("tm", 0),), 1)
    tile_tokens = TT * TH * TW
    tile_count = group_tokens // tile_tokens
    beside_all = beside_all.reshape(3, tile_count, tile_tokens, heads_here, 2, head_dim)
    position = lax.axis_index("tm")
    valid = jnp.stack([position > 0, position >= 0, position < lax.axis_size("tm") - 1])
    query_tiles = queries.reshape(tile_count, tile_tokens, heads_here, head_dim)

    def one_tile(item):
        block, picks = item
        return attend(block, jnp.take(beside_all, picks, axis=1), valid)

    attn = lax.map(one_tile, (query_tiles, window)).reshape(group_tokens, heads_here, head_dim)
    flat_attn = attn.reshape(group_tokens, heads_here * head_dim)
    flat_out = w_out.reshape(heads_here * head_dim, model_dim)
    product = jnp.dot(flat_attn, flat_out, preferred_element_type=jnp.float32)
    summed = lax.psum_scatter(
        lax.optimization_barrier(product.astype(jnp.bfloat16))
        .astype(jnp.float32)
        .astype(jnp.bfloat16),
        "space",
        scatter_dimension=0,
        tiled=True,
    )
    return summed[None]


def solution(mesh):
    in_specs = (
        P("tm", "space", None, None),
        P(None, "space", None),
        P("space", None, None),
        P(),
        P(),
        P("tm", None),
        P(),
    )
    out_specs = P("tm", "space", None)
    return jax.shard_map(
        per_device, mesh=mesh, in_specs=in_specs, out_specs=out_specs, check_vma=False
    )
```

```python
import functools
import math

import jax
import jax.numpy as jnp
from jax import lax
from jax.experimental import pallas as pl
from jax.experimental.pallas import tpu as pltpu
from jax.sharding import PartitionSpec as P

MESH = pl.DeviceIdType.MESH
TT = 4
TH = 8
TW = 8


def fused_kernel(
    n_tm,
    n_z,
    frame,
    x_ref,
    wq_ref,
    wo_ref,
    qg_ref,
    kg_ref,
    perm_ref,
    out_ref,
    xg,
    wall,
    inner_w,
    stage,
    place,
    kv,
    scores,
    attn,
    attn_in,
    part_out,
    part_in,
    wz_send,
    wz_recv,
    wt_send,
    wt_recv,
    x_send,
    x_recv,
    sib_send,
    sib_recv,
    kv_send,
    kv_recv,
    at_send,
    at_recv,
    pt_send,
    pt_recv,
    wq_send,
    wq_recv,
    wp_send,
    wp_recv,
    qkv_send,
    qkv_recv,
):
    tm = lax.axis_index("tm")
    space = lax.axis_index("space")
    z = space // 2
    core = space % 2
    sibling = z * 2 + 1 - core
    tokens, model = x_ref.shape
    shards = 2 * n_z
    group = shards * tokens
    hd = kv.shape[2] // 4
    quarter = model // n_tm
    inner = jnp.logical_and(z > 0, z < n_z - 1)
    outer = jnp.logical_not(inner)
    end_of = (z - 1) * (n_z - 1)
    inner_of = 1 + z // (n_z - 1)

    def remote(src, dst, send, recv, t, s):
        return pltpu.make_async_remote_copy(
            src_ref=src, dst_ref=dst, send_sem=send, recv_sem=recv,
            device_id=(t, s), device_id_type=MESH,
        )

    def rows_of(index, count):
        return pl.ds(pl.multiple_of(index * count, count), count)

    def w_ring(way, u, zz):
        target = z + 1 if way == 0 else z - 1
        block = wall.at[tm, rows_of(zz, hd)]
        return remote(block, block, wz_send.at[way, u], wz_recv.at[way, u], tm, target * 2 + core)

    def x_ring(way, u, zz):
        target = z + 1 if way == 0 else z - 1
        block = xg.at[zz * 2 + core]
        return remote(block, block, x_send.at[way, u], x_recv.at[way, u], tm, target * 2 + core)

    def w_peer(k, zz, owner):
        block = wall.at[owner, rows_of(zz, hd)]
        return remote(
            block, block, wt_send.at[k - 1, zz], wt_recv.at[k - 1, zz], (tm + k) % n_tm, space
        )

    def x_sibling(zz, side):
        block = xg.at[zz * 2 + side]
        return remote(block, block, sib_send.at[zz], sib_recv.at[zz], tm, sibling)

    def kv_copy(way, slot):
        target = tm - 1 if way == 0 else tm + 1
        rows = rows_of(slot, tokens)
        return remote(
            kv.at[0, rows, pl.ds(hd, 2 * hd)],
            kv.at[2 - way, rows, pl.ds(hd, 2 * hd)],
            kv_send.at[way, slot],
            kv_recv.at[way, slot],
            target,
            space,
        )

    def wq_inward():
        rows = rows_of(tm, quarter)
        return remote(
            wq_ref.at[rows], inner_w.at[rows], wq_send, wq_recv, tm, inner_of * 2 + core
        )

    def wq_peer(k, owner):
        block = inner_w.at[rows_of(owner, quarter)]
        return remote(
            block, block, wp_send.at[k - 1], wp_recv.at[k - 1], (tm + k) % n_tm, space
        )

    def qkv_outward(slot):
        return remote(
            stage.at[slot],
            kv.at[0, rows_of(slot, tokens), pl.ds(0, 3 * hd)],
            qkv_send.at[slot],
            qkv_recv.at[slot],
            tm,
            end_of * 2 + core,
        )

    def attn_copy(zz):
        return remote(
            attn.at[zz], attn_in.at[z], at_send.at[zz], at_recv.at[z], tm, zz * 2 + core
        )

    def attn_arrival(zz):
        return remote(
            attn.at[zz], attn_in.at[zz], at_send.at[zz], at_recv.at[zz], tm, zz * 2 + core
        )

    def part_copy(j):
        return remote(
            part_out.at[j], part_in.at[j], pt_send.at[j], pt_recv.at[j], tm, sibling
        )

    barrier = pltpu.get_barrier_semaphore()
    for k in range(1, n_z):
        pl.semaphore_signal(
            barrier, inc=1, device_id=(tm, (z + k) % n_z * 2 + core), device_id_type=MESH
        )
    for k in range(1, n_tm):
        pl.semaphore_signal(barrier, inc=1, device_id=((tm + k) % n_tm, space), device_id_type=MESH)
    pl.semaphore_signal(barrier, inc=1, device_id=(tm, sibling), device_id_type=MESH)
    for j in range(n_tm):
        wall[j, rows_of(z, hd), :] = wo_ref[:, j * quarter : (j + 1) * quarter]
    xg[space] = x_ref[...]
    kv[0, :, 3 * hd :] = jnp.ones((group, hd), jnp.bfloat16)
    pl.semaphore_wait(barrier, n_z - 1 + n_tm - 1 + 1)

    @pl.when(outer)
    def _():
        wq_inward().start()

    def norm(value, gain):
        scaled = value * lax.rsqrt(jnp.mean(value * value, axis=-1, keepdims=True) + 1e-06)
        return (scaled * gain).astype(jnp.bfloat16)

    def project(slot, weights):
        qkv = jnp.dot(xg[slot], weights[...], preferred_element_type=jnp.float32)
        qkv = qkv.astype(jnp.bfloat16)
        query = norm(qkv[:, :hd].astype(jnp.float32), qg_ref[...])
        key = norm(qkv[:, hd : 2 * hd].astype(jnp.float32), kg_ref[...])
        return jnp.concatenate([query, key, qkv[:, 2 * hd :]], axis=1)

    def inside(zz):
        return jnp.logical_and(zz >= 0, zz < n_z)

    def forwards_w(way):
        return z < n_z - 1 if way == 0 else z > 0

    def forwards_x(way):
        return z < n_z - 2 if way == 0 else z > 1

    def spread_w(u):
        for way in (0, 1):
            zz = z - u if way == 0 else z + u
            live = inside(zz)

            @pl.when(jnp.logical_and(live, u > 0))
            def _():
                w_ring(way, u - 1, zz).wait_recv()

            @pl.when(jnp.logical_and(live, forwards_w(way)))
            def _():
                w_ring(way, u, zz).start()

            @pl.when(jnp.logical_and(live, u > 0))
            def _():
                for k in range(1, n_tm):
                    w_peer(k, zz, tm).start()

    def pick_item(u, i):
        way = i % 2
        other = i // 2
        zz = z - u + way * 2 * u
        fresh = jnp.logical_and(inside(zz), way * (1 - jnp.minimum(u, 1)) == 0)
        return zz, other, zz * 2 + core + other * (1 - 2 * core), fresh

    def outward(u, carry):
        def item(i, carry):
            zz, other, slot, fresh = pick_item(u, i)

            @pl.when(jnp.logical_and(fresh, zz != end_of))
            def _():
                stage[slot] = project(slot, inner_w)
                qkv_outward(slot).start()

            return carry

        return lax.fori_loop(0, 4, item, carry)

    def step(u, carry):
        for way in (0, 1):
            zz = z - u if way == 0 else z + u
            live = jnp.logical_and(inside(zz), jnp.logical_or(inner, u == 0))
            fresh = live if way == 0 else jnp.logical_and(live, u > 0)

            @pl.when(jnp.logical_and(live, u > 0))
            def _():
                x_ring(way, u - 1, zz).wait_recv()

            @pl.when(jnp.logical_and(live, forwards_x(way)))
            def _():
                x_ring(way, u, zz).start()

            @pl.when(fresh)
            def _():
                x_sibling(zz, core).start()

        @pl.when(outer)
        def _():
            spread_w(u)

        def item(i, carry):
            zz, other, slot, fresh = pick_item(u, i)
            here = jnp.logical_or(inner, u == 0)

            @pl.when(jnp.logical_and(fresh, here))
            def _():
                @pl.when(other == 1)
                def _():
                    x_sibling(zz, 1 - core).wait_recv()

                kv[0, rows_of(slot, tokens), 0 : 3 * hd] = project(slot, wq_ref)

            @pl.when(jnp.logical_and(fresh, jnp.logical_not(here)))
            def _():
                qkv_outward(slot).wait_recv()

            @pl.when(jnp.logical_and(fresh, tm > 0))
            def _():
                kv_copy(0, slot).start()

            @pl.when(jnp.logical_and(fresh, tm < n_tm - 1))
            def _():
                kv_copy(1, slot).start()

            return carry

        lax.fori_loop(0, 4, item, 0)

        @pl.when(jnp.logical_and(inner, u == 0))
        def _():
            wq_inward().wait_recv()
            for k in range(1, n_tm):
                wq_peer(k, tm).start()

        @pl.when(inner)
        def _():
            spread_w(u)

        @pl.when(jnp.logical_and(inner, u == 1))
        def _():
            for k in range(1, n_tm):
                wq_peer(k, (tm + n_tm - k) % n_tm).wait_recv()

        @pl.when(jnp.logical_and(inner, jnp.logical_and(u > 0, u < n_z - 1)))
        def _():
            lax.fori_loop((u - 1) * 2, u + 1, outward, 0)

        return carry

    token = perm_ref[...].astype(jnp.float32)
    rows_here, cols, plane = frame

    def whole(value, by):
        return jnp.floor((value + 0.5) * (1.0 / by))

    at_frame = whole(token, plane)
    token = token - at_frame * plane
    row = whole(token, cols)
    col = token - row * cols
    shard = whole(row, rows_here)
    pos = shard * tokens + (at_frame * rows_here + row - shard * rows_here) * cols + col
    for i in range(group // hd):
        block = jnp.broadcast_to(pos[:, i * hd : (i + 1) * hd], (hd, hd))
        place[i * hd : (i + 1) * hd, :] = block.T

    lax.fori_loop(0, n_z, step, 0)

    for way in (0, 1):
        here = 2 - way
        live = tm < n_tm - 1 if way == 0 else tm > 0

        @pl.when(live)
        def _():
            kv[here, :, 3 * hd :] = jnp.ones((group, hd), jnp.bfloat16)

            def arrive(slot, carry):
                kv_copy(way, slot).wait_recv()
                return carry

            lax.fori_loop(0, shards, arrive, 0)

        @pl.when(jnp.logical_not(live))
        def _():
            kv[here, :, hd : 2 * hd] = kv[0, :, hd : 2 * hd]
            kv[here, :, 2 * hd :] = jnp.zeros((group, 2 * hd), jnp.bfloat16)

    factor = math.log2(math.e) * hd**-0.5
    block_rows = 2 * tokens

    def attend_block(i, carry):
        zz = (z + 1 + i) % n_z
        pos = place[rows_of(zz, block_rows), :]
        lanes = lax.broadcasted_iota(jnp.int32, (block_rows, hd), 1).astype(jnp.float32)
        picks = [jnp.where(pos - i * hd == lanes, 1.0, 0.0) for i in range(group // hd)]
        pick = jnp.concatenate([p.astype(jnp.bfloat16) for p in picks], axis=1)
        query = jnp.dot(pick, kv[0, :, 0:hd], preferred_element_type=jnp.float32)
        query = query.astype(jnp.bfloat16)
        highest = None
        for part in range(3):
            score = lax.dot_general(
                query,
                kv[part, :, hd : 2 * hd],
                (((1,), (1,)), ((), ())),
                preferred_element_type=jnp.float32,
            )
            scores[part] = score
            top = jnp.max(score, axis=-1, keepdims=True)
            highest = top if highest is None else jnp.maximum(highest, top)
        total = jnp.zeros((block_rows, 2 * hd), jnp.float32)
        for part in range(3):
            weights = jnp.exp2((scores[part] - highest) * factor).astype(jnp.bfloat16)
            total += jnp.dot(weights, kv[part, :, 2 * hd :], preferred_element_type=jnp.float32)
        result = (total[:, :hd] / total[:, hd:]).astype(jnp.bfloat16)

        @pl.when(zz == z)
        def _():
            attn_in[z] = result

        @pl.when(zz != z)
        def _():
            attn[zz] = result
            attn_copy(zz).start()

        return carry

    lax.fori_loop(0, n_z, attend_block, 0)

    def others(body):
        for k in range(1, n_z):
            body((z + k) % n_z)

    def weights_in(zz):
        for k in range(1, n_tm):
            w_peer(k, zz, (tm + n_tm - k) % n_tm).wait_recv()

    others(weights_in)
    others(lambda zz: attn_arrival(zz).wait_recv())

    def mixed(side, j):
        rows = rows_of(side, tokens)
        left = jnp.concatenate([attn_in[zz, rows, :] for zz in range(n_z)], axis=1)
        return jnp.dot(left, wall[j], preferred_element_type=jnp.float32)

    for j in range(n_tm):
        part_out[j] = mixed(1 - core, j).astype(jnp.bfloat16)
        part_copy(j).start()
    for j in range(n_tm):
        own = mixed(core, j)
        part_copy(j).wait_recv()
        total = own + part_in[j].astype(jnp.float32)
        out_ref[:, j * quarter : (j + 1) * quarter] = total.astype(jnp.bfloat16)

    for j in range(n_tm):
        part_copy(j).wait_send()

    def sent(zz):
        attn_copy(zz).wait_send()
        for k in range(1, n_tm):
            w_peer(k, zz, tm).wait_send()

    others(sent)

    def drain(slot, carry):
        @pl.when(tm > 0)
        def _():
            kv_copy(0, slot).wait_send()

        @pl.when(tm < n_tm - 1)
        def _():
            kv_copy(1, slot).wait_send()

        return carry

    lax.fori_loop(0, shards, drain, 0)
    for zz in range(n_z):

        @pl.when(jnp.logical_or(inner, zz == z))
        def _():
            x_sibling(zz, core).wait_send()

        @pl.when(jnp.logical_and(inner, zz != end_of))
        def _():
            for side in (0, 1):
                qkv_outward(zz * 2 + side).wait_send()
    for u in range(n_z - 1):
        for way in (0, 1):
            zz = z - u if way == 0 else z + u

            @pl.when(jnp.logical_and(inside(zz), forwards_w(way)))
            def _():
                w_ring(way, u, zz).wait_send()

            live = jnp.logical_and(inside(zz), jnp.logical_or(inner, u == 0))

            @pl.when(jnp.logical_and(live, forwards_x(way)))
            def _():
                x_ring(way, u, zz).wait_send()

    @pl.when(outer)
    def _():
        wq_inward().wait_send()

    @pl.when(inner)
    def _():
        for k in range(1, n_tm):
            wq_peer(k, tm).wait_send()


def fused(n_tm, n_z, frame, x, wq, wo, q_gain, k_gain, perm):
    tokens, model = x.shape
    hd = wo.shape[0]
    shards = 2 * n_z
    group = shards * tokens
    bf = jnp.bfloat16
    dma = pltpu.SemaphoreType.DMA
    vmem = pl.BlockSpec(memory_space=pltpu.VMEM)
    return pl.pallas_call(
        functools.partial(fused_kernel, n_tm, n_z, frame),
        out_shape=jax.ShapeDtypeStruct((tokens, model), bf),
        in_specs=[vmem] * 6,
        out_specs=vmem,
        scratch_shapes=[
            pltpu.VMEM((shards, tokens, model), bf),
            pltpu.VMEM((n_tm, n_z * hd, model // n_tm), bf),
            pltpu.VMEM((model, 3 * hd), bf),
            pltpu.VMEM((shards, tokens, 3 * hd), bf),
            pltpu.VMEM((group, hd), jnp.float32),
            pltpu.VMEM((3, group, 4 * hd), bf),
            pltpu.VMEM((3, 2 * tokens, group), jnp.float32),
            pltpu.VMEM((n_z, 2 * tokens, hd), bf),
            pltpu.VMEM((n_z, 2 * tokens, hd), bf),
            pltpu.VMEM((n_tm, tokens, model // n_tm), bf),
            pltpu.VMEM((n_tm, tokens, model // n_tm), bf),
            dma((2, n_z)),
            dma((2, n_z)),
            dma((n_tm - 1, n_z)),
            dma((n_tm - 1, n_z)),
            dma((2, n_z)),
            dma((2, n_z)),
            dma((n_z,)),
            dma((n_z,)),
            dma((2, shards)),
            dma((2, shards)),
            dma((n_z,)),
            dma((n_z,)),
            dma((n_tm,)),
            dma((n_tm,)),
            dma,
            dma,
            dma((n_tm - 1,)),
            dma((n_tm - 1,)),
            dma((shards,)),
            dma((shards,)),
        ],
        compiler_params=pltpu.CompilerParams(
            collective_id=0, has_side_effects=True, vmem_limit_bytes=56 * 1024 * 1024
        ),
    )(x, wq, wo, q_gain, k_gain, perm)


def whole_window(video, w_qkv, w_out, q_gain, k_gain, tile_perm):
    frames, rows_here, cols, model = video.shape
    n_tm = lax.axis_size("tm")
    n_space = lax.axis_size("space")
    hd = w_out.shape[1]
    tokens = frames * rows_here * cols
    mixed = fused(
        n_tm,
        n_space // 2,
        (rows_here, cols, rows_here * n_space * cols),
        video.reshape(tokens, model),
        w_qkv.reshape(model, 3 * hd),
        w_out.reshape(hd, model),
        q_gain.reshape(1, hd),
        k_gain.reshape(1, hd),
        tile_perm,
    )
    return mixed[None]


def extended(cells, sides, width):
    for axis, dim in sides:
        count = lax.axis_size(axis)
        ends = count - 1
        head = lax.slice_in_dim(cells, 0, width, axis=dim)
        tail = lax.slice_in_dim(cells, cells.shape[dim] - width, cells.shape[dim], axis=dim)
        cells = jnp.concatenate(
            [
                lax.ppermute(tail, axis, [(i, (i + 1) % count) for i in range(ends)]),
                cells,
                lax.ppermute(head, axis, [((i + 1) % count, i) for i in range(ends)]),
            ],
            axis=dim,
        )
    return cells


def head_norm(values, gain):
    wide = values.astype(jnp.float32)
    scaled = wide * lax.rsqrt(jnp.mean(wide * wide, axis=-1, keepdims=True) + 1e-06)
    return (scaled * gain).astype(jnp.bfloat16)


def attend(queries, chosen, valid):
    heads_here = queries.shape[1]
    head_dim = queries.shape[2]
    span = chosen.shape[1] * chosen.shape[2]
    keys = chosen[:, :, :, :, 0, :].reshape(-1, heads_here, head_dim)
    values = chosen[:, :, :, :, 1, :].reshape(-1, heads_here, head_dim)
    scores = jnp.einsum(
        "qhd,khd->hqk", queries, keys, preferred_element_type=jnp.float32
    ) * head_dim ** (-0.5)
    live = jnp.repeat(valid, span)
    scores = jnp.where(live[None, None, :], scores, -jnp.inf)
    highest = jnp.max(scores, axis=-1, keepdims=True)
    weights = jnp.exp(scores - highest)
    probs = (weights / jnp.sum(weights, axis=-1, keepdims=True)).astype(jnp.bfloat16)
    result = jnp.einsum("hqk,khd->qhd", probs, values, preferred_element_type=jnp.float32)
    return result.astype(jnp.bfloat16)


def per_device(video, w_qkv, w_out, q_gain, k_gain, tile_perm, window):
    tiles = video.shape[0] * video.shape[1] * lax.axis_size("space") * video.shape[2] // (TT * TH * TW)
    sized = lax.axis_size("tm") == 4 and lax.axis_size("space") == 8
    if window.shape[1] == tiles and w_qkv.shape[1] == 1 and sized:
        return whole_window(video, w_qkv, w_out, q_gain, k_gain, tile_perm)
    frames_here = video.shape[0]
    cols_here = video.shape[2]
    model_dim = video.shape[3]
    heads_here = w_qkv.shape[1]
    head_dim = w_out.shape[1]
    flat_w = w_qkv.reshape(model_dim, heads_here * 3 * head_dim)
    qkv = jnp.einsum(
        "frwd,dc->frwc",
        lax.all_gather(video, "space", axis=1, tiled=True),
        flat_w,
        preferred_element_type=jnp.float32,
    ).astype(jnp.bfloat16)
    group_tokens = frames_here * qkv.shape[1] * cols_here
    qkv = qkv.reshape(group_tokens, heads_here, 3, head_dim)
    ordered = jnp.take(qkv, tile_perm[0], axis=0)
    queries = head_norm(ordered[:, :, 0, :], q_gain)
    keys = head_norm(ordered[:, :, 1, :], k_gain)
    pairs = jnp.stack([keys, ordered[:, :, 2, :]], axis=2)
    beside_all = extended(pairs[None], (("tm", 0),), 1)
    tile_tokens = TT * TH * TW
    tile_count = group_tokens // tile_tokens
    beside_all = beside_all.reshape(3, tile_count, tile_tokens, heads_here, 2, head_dim)
    position = lax.axis_index("tm")
    valid = jnp.stack([position > 0, position >= 0, position < lax.axis_size("tm") - 1])
    query_tiles = queries.reshape(tile_count, tile_tokens, heads_here, head_dim)

    def one_tile(item):
        block, picks = item
        return attend(block, jnp.take(beside_all, picks, axis=1), valid)

    attn = lax.map(one_tile, (query_tiles, window)).reshape(group_tokens, heads_here, head_dim)
    flat_attn = attn.reshape(group_tokens, heads_here * head_dim)
    flat_out = w_out.reshape(heads_here * head_dim, model_dim)
    product = jnp.dot(flat_attn, flat_out, preferred_element_type=jnp.float32)
    summed = lax.psum_scatter(
        lax.optimization_barrier(product.astype(jnp.bfloat16))
        .astype(jnp.float32)
        .astype(jnp.bfloat16),
        "space",
        scatter_dimension=0,
        tiled=True,
    )
    return summed[None]


def solution(mesh):
    in_specs = (
        P("tm", "space", None, None),
        P(None, "space", None),
        P("space", None, None),
        P(),
        P(),
        P("tm", None),
        P(),
    )
    out_specs = P("tm", "space", None)
    return jax.shard_map(
        per_device, mesh=mesh, in_specs=in_specs, out_specs=out_specs, check_vma=False
    )
```

```python
import functools
import math

import jax
import jax.numpy as jnp
from jax import lax
from jax.experimental import pallas as pl
from jax.experimental.pallas import tpu as pltpu
from jax.sharding import PartitionSpec as P

MESH = pl.DeviceIdType.MESH
TT = 4
TH = 8
TW = 8


def fused_kernel(
    n_tm,
    n_z,
    frame,
    x_ref,
    wq_ref,
    wo_ref,
    qg_ref,
    kg_ref,
    perm_ref,
    out_ref,
    xg,
    wall,
    inner_w,
    stage,
    place,
    kv,
    scores,
    attn,
    attn_in,
    part_out,
    part_in,
    own,
    wz_send,
    wz_recv,
    wt_send,
    wt_recv,
    x_send,
    x_recv,
    sib_send,
    sib_recv,
    kv_send,
    kv_recv,
    at_send,
    at_recv,
    pt_send,
    pt_recv,
    wq_send,
    wq_recv,
    wp_send,
    wp_recv,
    qkv_send,
    qkv_recv,
):
    tm = lax.axis_index("tm")
    space = lax.axis_index("space")
    z = space // 2
    core = space % 2
    sibling = z * 2 + 1 - core
    tokens, model = x_ref.shape
    shards = 2 * n_z
    group = shards * tokens
    hd = kv.shape[2] // 4
    quarter = model // n_tm
    inner = jnp.logical_and(z > 0, z < n_z - 1)
    outer = jnp.logical_not(inner)
    end_of = (z - 1) * (n_z - 1)
    inner_of = 1 + z // (n_z - 1)

    def remote(src, dst, send, recv, t, s):
        return pltpu.make_async_remote_copy(
            src_ref=src, dst_ref=dst, send_sem=send, recv_sem=recv,
            device_id=(t, s), device_id_type=MESH,
        )

    def rows_of(index, count):
        return pl.ds(pl.multiple_of(index * count, count), count)

    def w_ring(way, u, zz):
        target = z + 1 if way == 0 else z - 1
        block = wall.at[tm, rows_of(zz, hd)]
        return remote(block, block, wz_send.at[way, u], wz_recv.at[way, u], tm, target * 2 + core)

    def x_ring(way, u, zz, part):
        target = z + 1 if way == 0 else z - 1
        block = xg.at[zz * 2 + core, pl.ds(part * (tokens // 2), tokens // 2)]
        return remote(
            block, block, x_send.at[way, u, part], x_recv.at[way, u, part], tm, target * 2 + core
        )

    def w_peer(k, zz, owner):
        block = wall.at[owner, rows_of(zz, hd)]
        return remote(
            block, block, wt_send.at[k - 1, zz], wt_recv.at[k - 1, zz], (tm + k) % n_tm, space
        )

    def x_sibling(zz, side):
        block = xg.at[zz * 2 + side]
        return remote(block, block, sib_send.at[zz], sib_recv.at[zz], tm, sibling)

    def kv_copy(way, slot):
        target = tm - 1 if way == 0 else tm + 1
        rows = rows_of(slot, tokens)
        return remote(
            kv.at[0, rows, pl.ds(hd, 2 * hd)],
            kv.at[2 - way, rows, pl.ds(hd, 2 * hd)],
            kv_send.at[way, slot],
            kv_recv.at[way, slot],
            target,
            space,
        )

    def wq_inward():
        rows = rows_of(tm, quarter)
        return remote(
            wq_ref.at[rows], inner_w.at[rows], wq_send, wq_recv, tm, inner_of * 2 + core
        )

    beside = tm + 1 - 2 * (tm % 2)
    across = (tm + n_tm // 2) % n_tm

    def wq_peer(k, owner):
        block = inner_w.at[rows_of(owner, quarter)]
        target = beside if k == 0 else across
        return remote(block, block, wp_send.at[k], wp_recv.at[k], target, space)

    def qkv_outward(slot):
        return remote(
            stage.at[slot],
            kv.at[0, rows_of(slot, tokens), pl.ds(0, 3 * hd)],
            qkv_send.at[slot],
            qkv_recv.at[slot],
            tm,
            end_of * 2 + core,
        )

    def attn_copy(zz):
        return remote(
            attn.at[zz], attn_in.at[z], at_send.at[zz], at_recv.at[z], tm, zz * 2 + core
        )

    def attn_arrival(zz):
        return remote(
            attn.at[zz], attn_in.at[zz], at_send.at[zz], at_recv.at[zz], tm, zz * 2 + core
        )

    def part_copy(j):
        return remote(
            part_out.at[j], part_in.at[j], pt_send.at[j], pt_recv.at[j], tm, sibling
        )

    barrier = pltpu.get_barrier_semaphore()
    for k in range(1, n_z):
        pl.semaphore_signal(
            barrier, inc=1, device_id=(tm, (z + k) % n_z * 2 + core), device_id_type=MESH
        )
    for k in range(1, n_tm):
        pl.semaphore_signal(barrier, inc=1, device_id=((tm + k) % n_tm, space), device_id_type=MESH)
    pl.semaphore_signal(barrier, inc=1, device_id=(tm, sibling), device_id_type=MESH)
    for j in range(n_tm):
        wall[j, rows_of(z, hd), :] = wo_ref[:, j * quarter : (j + 1) * quarter]
    xg[space] = x_ref[...]
    kv[0, :, 3 * hd :] = jnp.ones((group, hd), jnp.bfloat16)
    pl.semaphore_wait(barrier, n_z - 1 + n_tm - 1 + 1)

    def norm(value, gain):
        scaled = value * lax.rsqrt(jnp.mean(value * value, axis=-1, keepdims=True) + 1e-06)
        return (scaled * gain).astype(jnp.bfloat16)

    def project(slot, weights):
        qkv = jnp.dot(xg[slot], weights[...], preferred_element_type=jnp.float32)
        qkv = qkv.astype(jnp.bfloat16)
        query = norm(qkv[:, :hd].astype(jnp.float32), qg_ref[...])
        key = norm(qkv[:, hd : 2 * hd].astype(jnp.float32), kg_ref[...])
        return jnp.concatenate([query, key, qkv[:, 2 * hd :]], axis=1)

    def inside(zz):
        return jnp.logical_and(zz >= 0, zz < n_z)

    def forwards_w(way):
        return z < n_z - 1 if way == 0 else z > 0

    def forwards_x(way):
        return z < n_z - 2 if way == 0 else z > 1

    def spread_w(u):
        for way in (0, 1):
            zz = z - u if way == 0 else z + u
            live = inside(zz)

            @pl.when(jnp.logical_and(live, u > 0))
            def _():
                w_ring(way, u - 1, zz).wait_recv()

            @pl.when(jnp.logical_and(live, forwards_w(way)))
            def _():
                w_ring(way, u, zz).start()

    def pick_item(u, i):
        way = i % 2
        other = i // 2
        zz = z - u + way * 2 * u
        fresh = jnp.logical_and(inside(zz), way * (1 - jnp.minimum(u, 1)) == 0)
        return zz, other, zz * 2 + core + other * (1 - 2 * core), fresh

    def outward(u, carry):
        def item(i, carry):
            zz, other, slot, fresh = pick_item(u, i)

            @pl.when(jnp.logical_and(fresh, zz != end_of))
            def _():
                stage[slot] = project(slot, inner_w)
                qkv_outward(slot).start()

            return carry

        return lax.fori_loop(0, 4, item, carry)

    def step(u, carry):
        def arrive(part):
            for way in (0, 1):
                zz = z - u if way == 0 else z + u

                @pl.when(jnp.logical_and(jnp.logical_and(inside(zz), inner), u > 0))
                def _():
                    x_ring(way, u - 1, zz, part).wait_recv()

                @pl.when(jnp.logical_and(jnp.logical_and(inside(zz), inner), forwards_x(way)))
                def _():
                    x_ring(way, u, zz, part).start()

        for way in (0, 1):

            @pl.when(jnp.logical_and(jnp.logical_and(outer, u == 0), forwards_x(way)))
            def _():
                x_ring(way, u, z, 0).start()

        arrive(0)

        @pl.when(jnp.logical_and(inner, u == 1))
        def _():
            wq_inward().wait_recv()
            for k in (0, 1):
                wq_peer(k, tm).start()

        arrive(1)

        @pl.when(jnp.logical_and(inner, u == 1))
        def _():
            wq_peer(0, beside).wait_recv()
            wq_peer(2, beside).start()

        for way in (0, 1):
            zz = z - u if way == 0 else z + u
            live = jnp.logical_and(inside(zz), jnp.logical_or(inner, u == 0))
            fresh = live if way == 0 else jnp.logical_and(live, u > 0)

            @pl.when(fresh)
            def _():
                x_sibling(zz, core).start()

        @pl.when(outer)
        def _():
            spread_w(u)

        def item(i, carry):
            zz, other, slot, fresh = pick_item(u, i)
            here = jnp.logical_or(inner, u == 0)

            @pl.when(jnp.logical_and(fresh, here))
            def _():
                @pl.when(other == 1)
                def _():
                    x_sibling(zz, 1 - core).wait_recv()

                kv[0, rows_of(slot, tokens), 0 : 3 * hd] = project(slot, wq_ref)

            @pl.when(jnp.logical_and(fresh, jnp.logical_not(here)))
            def _():
                qkv_outward(slot).wait_recv()

            @pl.when(jnp.logical_and(fresh, tm > 0))
            def _():
                kv_copy(0, slot).start()

            @pl.when(jnp.logical_and(fresh, tm < n_tm - 1))
            def _():
                kv_copy(1, slot).start()

            return carry

        lax.fori_loop(0, 4, item, 0)

        for way in (0, 1):

            @pl.when(jnp.logical_and(jnp.logical_and(outer, u == 0), forwards_x(way)))
            def _():
                x_ring(way, u, z, 0).wait_send()
                wq_inward().start()
                wq_inward().wait_send()
                x_ring(way, u, z, 1).start()

        @pl.when(inner)
        def _():
            spread_w(u)

        @pl.when(jnp.logical_and(inner, u == 1))
        def _():
            wq_peer(1, across).wait_recv()
            wq_peer(2, (beside + n_tm // 2) % n_tm).wait_recv()

        @pl.when(jnp.logical_and(inner, jnp.logical_and(u > 0, u < n_z - 1)))
        def _():
            lax.fori_loop((u - 1) * 2, u + 1, outward, 0)

        return carry

    token = perm_ref[...].astype(jnp.float32)
    rows_here, cols, plane = frame

    def whole(value, by):
        return jnp.floor((value + 0.5) * (1.0 / by))

    at_frame = whole(token, plane)
    token = token - at_frame * plane
    row = whole(token, cols)
    col = token - row * cols
    shard = whole(row, rows_here)
    pos = shard * tokens + (at_frame * rows_here + row - shard * rows_here) * cols + col
    for i in range(group // hd):
        block = jnp.broadcast_to(pos[:, i * hd : (i + 1) * hd], (hd, hd))
        place[i * hd : (i + 1) * hd, :] = block.T

    lax.fori_loop(0, n_z, step, 0)

    def others(body):
        for k in range(1, n_z):
            body((z + k) % n_z)

    def weights_out(zz):
        for k in range(1, n_tm):
            w_peer(k, zz, tm).start()

    others(weights_out)

    for way in (0, 1):
        here = 2 - way
        live = tm < n_tm - 1 if way == 0 else tm > 0

        @pl.when(live)
        def _():
            kv[here, :, 3 * hd :] = jnp.ones((group, hd), jnp.bfloat16)

            def arrive(slot, carry):
                kv_copy(way, slot).wait_recv()
                return carry

            lax.fori_loop(0, shards, arrive, 0)

        @pl.when(jnp.logical_not(live))
        def _():
            kv[here, :, hd : 2 * hd] = kv[0, :, hd : 2 * hd]
            kv[here, :, 2 * hd :] = jnp.zeros((group, 2 * hd), jnp.bfloat16)

    factor = math.log2(math.e) * hd**-0.5
    block_rows = 2 * tokens

    def attend_block(i, carry):
        zz = (z + 1 + i) % n_z
        pos = place[rows_of(zz, block_rows), :]
        lanes = lax.broadcasted_iota(jnp.int32, (block_rows, hd), 1).astype(jnp.float32)
        picks = [jnp.where(pos - i * hd == lanes, 1.0, 0.0) for i in range(group // hd)]
        pick = jnp.concatenate([p.astype(jnp.bfloat16) for p in picks], axis=1)
        query = jnp.dot(pick, kv[0, :, 0:hd], preferred_element_type=jnp.float32)
        query = query.astype(jnp.bfloat16)
        highest = None
        for part in range(3):
            score = lax.dot_general(
                query,
                kv[part, :, hd : 2 * hd],
                (((1,), (1,)), ((), ())),
                preferred_element_type=jnp.float32,
            )
            scores[part] = score
            top = jnp.max(score, axis=-1, keepdims=True)
            highest = top if highest is None else jnp.maximum(highest, top)
        total = jnp.zeros((block_rows, 2 * hd), jnp.float32)
        for part in range(3):
            weights = jnp.exp2((scores[part] - highest) * factor).astype(jnp.bfloat16)
            total += jnp.dot(weights, kv[part, :, 2 * hd :], preferred_element_type=jnp.float32)
        result = (total[:, :hd] / total[:, hd:]).astype(jnp.bfloat16)

        @pl.when(zz == z)
        def _():
            attn_in[z] = result

        @pl.when(zz != z)
        def _():
            attn[zz] = result
            attn_copy(zz).start()

        return carry

    lax.fori_loop(0, n_z, attend_block, 0)

    def weights_in(zz):
        for k in range(1, n_tm):
            w_peer(k, zz, (tm + n_tm - k) % n_tm).wait_recv()

    others(weights_in)
    others(lambda zz: attn_arrival(zz).wait_recv())

    def heads(side):
        rows = rows_of(side, tokens)
        return jnp.concatenate([attn_in[zz, rows, :] for zz in range(n_z)], axis=1)

    left = jnp.concatenate([heads(1 - core), heads(core)], axis=0)
    for j in range(n_tm):
        both = jnp.dot(left, wall[j], preferred_element_type=jnp.float32)
        part_out[j] = both[:tokens].astype(jnp.bfloat16)
        part_copy(j).start()
        own[j] = both[tokens:]
    for j in range(n_tm):
        part_copy(j).wait_recv()
        total = own[j] + part_in[j].astype(jnp.float32)
        out_ref[:, j * quarter : (j + 1) * quarter] = total.astype(jnp.bfloat16)

    for j in range(n_tm):
        part_copy(j).wait_send()

    def sent(zz):
        attn_copy(zz).wait_send()
        for k in range(1, n_tm):
            w_peer(k, zz, tm).wait_send()

    others(sent)

    def drain(slot, carry):
        @pl.when(tm > 0)
        def _():
            kv_copy(0, slot).wait_send()

        @pl.when(tm < n_tm - 1)
        def _():
            kv_copy(1, slot).wait_send()

        return carry

    lax.fori_loop(0, shards, drain, 0)
    for zz in range(n_z):

        @pl.when(jnp.logical_or(inner, zz == z))
        def _():
            x_sibling(zz, core).wait_send()

        @pl.when(jnp.logical_and(inner, zz != end_of))
        def _():
            for side in (0, 1):
                qkv_outward(zz * 2 + side).wait_send()
    for u in range(n_z - 1):
        for way in (0, 1):
            zz = z - u if way == 0 else z + u

            @pl.when(jnp.logical_and(inside(zz), forwards_w(way)))
            def _():
                w_ring(way, u, zz).wait_send()

            for part in (0, 1):
                live = inner if part == 0 else jnp.logical_or(inner, u == 0)

                @pl.when(jnp.logical_and(jnp.logical_and(live, inside(zz)), forwards_x(way)))
                def _():
                    x_ring(way, u, zz, part).wait_send()

    @pl.when(inner)
    def _():
        wq_peer(0, tm).wait_send()
        wq_peer(1, tm).wait_send()
        wq_peer(2, beside).wait_send()


def fused(n_tm, n_z, frame, x, wq, wo, q_gain, k_gain, perm):
    tokens, model = x.shape
    hd = wo.shape[0]
    shards = 2 * n_z
    group = shards * tokens
    bf = jnp.bfloat16
    dma = pltpu.SemaphoreType.DMA
    vmem = pl.BlockSpec(memory_space=pltpu.VMEM)
    return pl.pallas_call(
        functools.partial(fused_kernel, n_tm, n_z, frame),
        out_shape=jax.ShapeDtypeStruct((tokens, model), bf),
        in_specs=[vmem] * 6,
        out_specs=vmem,
        scratch_shapes=[
            pltpu.VMEM((shards, tokens, model), bf),
            pltpu.VMEM((n_tm, n_z * hd, model // n_tm), bf),
            pltpu.VMEM((model, 3 * hd), bf),
            pltpu.VMEM((shards, tokens, 3 * hd), bf),
            pltpu.VMEM((group, hd), jnp.float32),
            pltpu.VMEM((3, group, 4 * hd), bf),
            pltpu.VMEM((3, 2 * tokens, group), jnp.float32),
            pltpu.VMEM((n_z, 2 * tokens, hd), bf),
            pltpu.VMEM((n_z, 2 * tokens, hd), bf),
            pltpu.VMEM((n_tm, tokens, model // n_tm), bf),
            pltpu.VMEM((n_tm, tokens, model // n_tm), bf),
            pltpu.VMEM((n_tm, tokens, model // n_tm), jnp.float32),
            dma((2, n_z)),
            dma((2, n_z)),
            dma((n_tm - 1, n_z)),
            dma((n_tm - 1, n_z)),
            dma((2, n_z, 2)),
            dma((2, n_z, 2)),
            dma((n_z,)),
            dma((n_z,)),
            dma((2, shards)),
            dma((2, shards)),
            dma((n_z,)),
            dma((n_z,)),
            dma((n_tm,)),
            dma((n_tm,)),
            dma,
            dma,
            dma((n_tm - 1,)),
            dma((n_tm - 1,)),
            dma((shards,)),
            dma((shards,)),
        ],
        compiler_params=pltpu.CompilerParams(
            collective_id=0, has_side_effects=True, vmem_limit_bytes=56 * 1024 * 1024
        ),
    )(x, wq, wo, q_gain, k_gain, perm)


def whole_window(video, w_qkv, w_out, q_gain, k_gain, tile_perm):
    frames, rows_here, cols, model = video.shape
    n_tm = lax.axis_size("tm")
    n_space = lax.axis_size("space")
    hd = w_out.shape[1]
    tokens = frames * rows_here * cols
    mixed = fused(
        n_tm,
        n_space // 2,
        (rows_here, cols, rows_here * n_space * cols),
        video.reshape(tokens, model),
        w_qkv.reshape(model, 3 * hd),
        w_out.reshape(hd, model),
        q_gain.reshape(1, hd),
        k_gain.reshape(1, hd),
        tile_perm,
    )
    return mixed[None]


def extended(cells, sides, width):
    for axis, dim in sides:
        count = lax.axis_size(axis)
        ends = count - 1
        head = lax.slice_in_dim(cells, 0, width, axis=dim)
        tail = lax.slice_in_dim(cells, cells.shape[dim] - width, cells.shape[dim], axis=dim)
        cells = jnp.concatenate(
            [
                lax.ppermute(tail, axis, [(i, (i + 1) % count) for i in range(ends)]),
                cells,
                lax.ppermute(head, axis, [((i + 1) % count, i) for i in range(ends)]),
            ],
            axis=dim,
        )
    return cells


def head_norm(values, gain):
    wide = values.astype(jnp.float32)
    scaled = wide * lax.rsqrt(jnp.mean(wide * wide, axis=-1, keepdims=True) + 1e-06)
    return (scaled * gain).astype(jnp.bfloat16)


def attend(queries, chosen, valid):
    heads_here = queries.shape[1]
    head_dim = queries.shape[2]
    span = chosen.shape[1] * chosen.shape[2]
    keys = chosen[:, :, :, :, 0, :].reshape(-1, heads_here, head_dim)
    values = chosen[:, :, :, :, 1, :].reshape(-1, heads_here, head_dim)
    scores = jnp.einsum(
        "qhd,khd->hqk", queries, keys, preferred_element_type=jnp.float32
    ) * head_dim ** (-0.5)
    live = jnp.repeat(valid, span)
    scores = jnp.where(live[None, None, :], scores, -jnp.inf)
    highest = jnp.max(scores, axis=-1, keepdims=True)
    weights = jnp.exp(scores - highest)
    probs = (weights / jnp.sum(weights, axis=-1, keepdims=True)).astype(jnp.bfloat16)
    result = jnp.einsum("hqk,khd->qhd", probs, values, preferred_element_type=jnp.float32)
    return result.astype(jnp.bfloat16)


def per_device(video, w_qkv, w_out, q_gain, k_gain, tile_perm, window):
    tiles = video.shape[0] * video.shape[1] * lax.axis_size("space") * video.shape[2] // (TT * TH * TW)
    sized = lax.axis_size("tm") == 4 and lax.axis_size("space") == 8
    if window.shape[1] == tiles and w_qkv.shape[1] == 1 and sized:
        return whole_window(video, w_qkv, w_out, q_gain, k_gain, tile_perm)
    frames_here = video.shape[0]
    cols_here = video.shape[2]
    model_dim = video.shape[3]
    heads_here = w_qkv.shape[1]
    head_dim = w_out.shape[1]
    flat_w = w_qkv.reshape(model_dim, heads_here * 3 * head_dim)
    qkv = jnp.einsum(
        "frwd,dc->frwc",
        lax.all_gather(video, "space", axis=1, tiled=True),
        flat_w,
        preferred_element_type=jnp.float32,
    ).astype(jnp.bfloat16)
    group_tokens = frames_here * qkv.shape[1] * cols_here
    qkv = qkv.reshape(group_tokens, heads_here, 3, head_dim)
    ordered = jnp.take(qkv, tile_perm[0], axis=0)
    queries = head_norm(ordered[:, :, 0, :], q_gain)
    keys = head_norm(ordered[:, :, 1, :], k_gain)
    pairs = jnp.stack([keys, ordered[:, :, 2, :]], axis=2)
    beside_all = extended(pairs[None], (("tm", 0),), 1)
    tile_tokens = TT * TH * TW
    tile_count = group_tokens // tile_tokens
    beside_all = beside_all.reshape(3, tile_count, tile_tokens, heads_here, 2, head_dim)
    position = lax.axis_index("tm")
    valid = jnp.stack([position > 0, position >= 0, position < lax.axis_size("tm") - 1])
    query_tiles = queries.reshape(tile_count, tile_tokens, heads_here, head_dim)

    def one_tile(item):
        block, picks = item
        return attend(block, jnp.take(beside_all, picks, axis=1), valid)

    attn = lax.map(one_tile, (query_tiles, window)).reshape(group_tokens, heads_here, head_dim)
    flat_attn = attn.reshape(group_tokens, heads_here * head_dim)
    flat_out = w_out.reshape(heads_here * head_dim, model_dim)
    product = jnp.dot(flat_attn, flat_out, preferred_element_type=jnp.float32)
    summed = lax.psum_scatter(
        lax.optimization_barrier(product.astype(jnp.bfloat16))
        .astype(jnp.float32)
        .astype(jnp.bfloat16),
        "space",
        scatter_dimension=0,
        tiled=True,
    )
    return summed[None]


def solution(mesh):
    in_specs = (
        P("tm", "space", None, None),
        P(None, "space", None),
        P("space", None, None),
        P(),
        P(),
        P("tm", None),
        P(),
    )
    out_specs = P("tm", "space", None)
    return jax.shard_map(
        per_device, mesh=mesh, in_specs=in_specs, out_specs=out_specs, check_vma=False
    )
```

```python
import functools
import math

import jax
import jax.numpy as jnp
from jax import lax
from jax.experimental import pallas as pl
from jax.experimental.pallas import tpu as pltpu
from jax.sharding import PartitionSpec as P

MESH = pl.DeviceIdType.MESH
TT = 4
TH = 8
TW = 8


def fused_kernel(
    n_tm,
    n_z,
    frame,
    x_ref,
    wq_ref,
    wo_ref,
    qg_ref,
    kg_ref,
    perm_ref,
    out_ref,
    xg,
    wall,
    inner_w,
    stage,
    place,
    kv,
    scores,
    attn,
    attn_in,
    part_out,
    part_in,
    own,
    wz_send,
    wz_recv,
    wt_send,
    wt_recv,
    x_send,
    x_recv,
    sib_send,
    sib_recv,
    kv_send,
    kv_recv,
    at_send,
    at_recv,
    pt_send,
    pt_recv,
    wq_send,
    wq_recv,
    wp_send,
    wp_recv,
    qkv_send,
    qkv_recv,
):
    tm = lax.axis_index("tm")
    space = lax.axis_index("space")
    z = space // 2
    core = space % 2
    sibling = z * 2 + 1 - core
    tokens, model = x_ref.shape
    shards = 2 * n_z
    group = shards * tokens
    hd = kv.shape[2] // 4
    quarter = model // n_tm
    inner = jnp.logical_and(z > 0, z < n_z - 1)
    outer = jnp.logical_not(inner)
    end_of = (z - 1) * (n_z - 1)
    inner_of = 1 + z // (n_z - 1)

    def remote(src, dst, send, recv, t, s):
        return pltpu.make_async_remote_copy(
            src_ref=src, dst_ref=dst, send_sem=send, recv_sem=recv,
            device_id=(t, s), device_id_type=MESH,
        )

    def rows_of(index, count):
        return pl.ds(pl.multiple_of(index * count, count), count)

    def w_ring(way, u, zz):
        target = z + 1 if way == 0 else z - 1
        block = wall.at[tm, rows_of(zz, hd)]
        return remote(block, block, wz_send.at[way, u], wz_recv.at[way, u], tm, target * 2 + core)

    def x_ring(way, u, zz, part):
        target = z + 1 if way == 0 else z - 1
        block = xg.at[zz * 2 + core, pl.ds(part * (tokens // 2), tokens // 2)]
        return remote(
            block, block, x_send.at[way, u, part], x_recv.at[way, u, part], tm, target * 2 + core
        )

    def w_peer(k, zz, owner):
        block = wall.at[owner, rows_of(zz, hd)]
        return remote(
            block, block, wt_send.at[k - 1, zz], wt_recv.at[k - 1, zz], (tm + k) % n_tm, space
        )

    def x_sibling(zz, side):
        block = xg.at[zz * 2 + side]
        return remote(block, block, sib_send.at[zz], sib_recv.at[zz], tm, sibling)

    def kv_copy(way, zz):
        target = tm - 1 if way == 0 else tm + 1
        rows = rows_of(zz, 2 * tokens)
        return remote(
            kv.at[0, rows, pl.ds(hd, 2 * hd)],
            kv.at[2 - way, rows, pl.ds(hd, 2 * hd)],
            kv_send.at[way, zz],
            kv_recv.at[way, zz],
            target,
            space,
        )

    def wq_inward():
        rows = rows_of(tm, quarter)
        return remote(
            wq_ref.at[rows], inner_w.at[rows], wq_send, wq_recv, tm, inner_of * 2 + core
        )

    beside = tm + 1 - 2 * (tm % 2)
    across = (tm + n_tm // 2) % n_tm

    def wq_peer(k, owner):
        block = inner_w.at[rows_of(owner, quarter)]
        target = beside if k == 0 else across
        return remote(block, block, wp_send.at[k], wp_recv.at[k], target, space)

    def qkv_outward(zz):
        return remote(
            stage,
            kv.at[0, rows_of(zz, 2 * tokens), pl.ds(0, 3 * hd)],
            qkv_send,
            qkv_recv,
            tm,
            end_of * 2 + core,
        )

    def attn_copy(zz):
        return remote(
            attn.at[zz], attn_in.at[z], at_send.at[zz], at_recv.at[z], tm, zz * 2 + core
        )

    def attn_arrival(zz):
        return remote(
            attn.at[zz], attn_in.at[zz], at_send.at[zz], at_recv.at[zz], tm, zz * 2 + core
        )

    def part_copy(j):
        return remote(
            part_out.at[j], part_in.at[j], pt_send.at[j], pt_recv.at[j], tm, sibling
        )

    barrier = pltpu.get_barrier_semaphore()
    for k in range(1, n_z):
        pl.semaphore_signal(
            barrier, inc=1, device_id=(tm, (z + k) % n_z * 2 + core), device_id_type=MESH
        )
    for k in range(1, n_tm):
        pl.semaphore_signal(barrier, inc=1, device_id=((tm + k) % n_tm, space), device_id_type=MESH)
    pl.semaphore_signal(barrier, inc=1, device_id=(tm, sibling), device_id_type=MESH)
    for j in range(n_tm):
        wall[j, rows_of(z, hd), :] = wo_ref[:, j * quarter : (j + 1) * quarter]
    xg[space] = x_ref[...]
    kv[0, :, 3 * hd :] = jnp.ones((group, hd), jnp.bfloat16)
    pl.semaphore_wait(barrier, n_z - 1 + n_tm - 1 + 1)

    def norm(value, gain):
        scaled = value * lax.rsqrt(jnp.mean(value * value, axis=-1, keepdims=True) + 1e-06)
        return (scaled * gain).astype(jnp.bfloat16)

    def project(zz, weights):
        both = xg[rows_of(zz, 2)].reshape(2 * tokens, model)
        qkv = jnp.dot(both, weights[...], preferred_element_type=jnp.float32)
        qkv = qkv.astype(jnp.bfloat16)
        query = norm(qkv[:, :hd].astype(jnp.float32), qg_ref[...])
        key = norm(qkv[:, hd : 2 * hd].astype(jnp.float32), kg_ref[...])
        return jnp.concatenate([query, key, qkv[:, 2 * hd :]], axis=1)

    def inside(zz):
        return jnp.logical_and(zz >= 0, zz < n_z)

    def forwards_w(way):
        return z < n_z - 1 if way == 0 else z > 0

    def spread_w(u):
        for way in (0, 1):
            zz = z - u if way == 0 else z + u
            live = inside(zz)

            @pl.when(jnp.logical_and(live, u > 0))
            def _():
                w_ring(way, u - 1, zz).wait_recv()

            @pl.when(jnp.logical_and(live, forwards_w(way)))
            def _():
                w_ring(way, u, zz).start()

            @pl.when(jnp.logical_and(jnp.logical_and(live, outer), u > 0))
            def _():
                for k in range(1, n_tm):
                    w_peer(k, zz, tm).start()

    def step(u, carry):
        def arrive(part):
            for way in (0, 1):
                zz = z - u if way == 0 else z + u

                @pl.when(jnp.logical_and(inside(zz), jnp.logical_and(u > 0, u < n_z - 1)))
                def _():
                    x_ring(way, u - 1, zz, part).wait_recv()

                going = jnp.logical_and(jnp.logical_or(inner, u >= part), u < n_z - 2)

                @pl.when(jnp.logical_and(jnp.logical_and(inside(zz), going), forwards_w(way)))
                def _():
                    x_ring(way, u, zz, part).start()

        arrive(0)

        @pl.when(jnp.logical_and(inner, u == 1))
        def _():
            wq_inward().wait_recv()
            for k in (0, 1):
                wq_peer(k, tm).start()

        arrive(1)

        @pl.when(jnp.logical_and(inner, u == 1))
        def _():
            wq_peer(0, beside).wait_recv()
            wq_peer(2, beside).start()

        for way in (0, 1):
            zz = z - u if way == 0 else z + u
            live = jnp.logical_and(inside(zz), u < n_z - 1)
            fresh = live if way == 0 else jnp.logical_and(live, u > 0)

            @pl.when(fresh)
            def _():
                x_sibling(zz, core).start()

        @pl.when(outer)
        def _():
            spread_w(u)

        def item(way, carry):
            zz = z - u + way * 2 * u
            fresh = jnp.logical_and(inside(zz), way * (1 - jnp.minimum(u, 1)) == 0)

            @pl.when(jnp.logical_and(fresh, u < n_z - 1))
            def _():
                x_sibling(zz, 1 - core).wait_recv()
                kv[0, rows_of(zz, 2 * tokens), 0 : 3 * hd] = project(zz, wq_ref)

            @pl.when(jnp.logical_and(fresh, u == n_z - 1))
            def _():
                qkv_outward(zz).wait_recv()

            @pl.when(jnp.logical_and(fresh, tm > 0))
            def _():
                kv_copy(0, zz).start()

            @pl.when(jnp.logical_and(fresh, tm < n_tm - 1))
            def _():
                kv_copy(1, zz).start()

            return carry

        lax.fori_loop(0, 2, item, 0)

        for way in (0, 1):

            @pl.when(jnp.logical_and(jnp.logical_and(outer, u == 0), forwards_w(way)))
            def _():
                x_ring(way, u, z, 0).wait_send()
                wq_inward().start()
                wq_inward().wait_send()
                x_ring(way, u, z, 1).start()

        @pl.when(inner)
        def _():
            spread_w(u)

        @pl.when(jnp.logical_and(inner, u == n_z - 2))
        def _():
            wq_peer(1, across).wait_recv()
            wq_peer(2, (beside + n_tm // 2) % n_tm).wait_recv()
            far = n_z - 1 - end_of
            stage[...] = project(far, inner_w)
            qkv_outward(far).start()

        return carry

    token = perm_ref[...].astype(jnp.float32)
    rows_here, cols, plane = frame

    def whole(value, by):
        return jnp.floor((value + 0.5) * (1.0 / by))

    at_frame = whole(token, plane)
    token = token - at_frame * plane
    row = whole(token, cols)
    col = token - row * cols
    shard = whole(row, rows_here)
    pos = shard * tokens + (at_frame * rows_here + row - shard * rows_here) * cols + col
    for i in range(group // hd):
        block = jnp.broadcast_to(pos[:, i * hd : (i + 1) * hd], (hd, hd))
        place[i * hd : (i + 1) * hd, :] = block.T

    lax.fori_loop(0, n_z, step, 0)

    def others(body):
        for k in range(1, n_z):
            body((z + k) % n_z)

    def weights_out(zz):
        for k in range(1, n_tm):
            w_peer(k, zz, tm).start()

    @pl.when(inner)
    def _():
        others(weights_out)

    for way in (0, 1):
        here = 2 - way
        live = tm < n_tm - 1 if way == 0 else tm > 0

        @pl.when(live)
        def _():
            kv[here, :, 3 * hd :] = jnp.ones((group, hd), jnp.bfloat16)

            for zz in range(n_z):
                kv_copy(way, zz).wait_recv()

        @pl.when(jnp.logical_not(live))
        def _():
            kv[here, :, hd : 2 * hd] = kv[0, :, hd : 2 * hd]
            kv[here, :, 2 * hd :] = jnp.zeros((group, 2 * hd), jnp.bfloat16)

    factor = math.log2(math.e) * hd**-0.5
    block_rows = 2 * tokens

    def attend_block(i, carry):
        zz = (z + 1 + i) % n_z
        pos = place[rows_of(zz, block_rows), :]
        lanes = lax.broadcasted_iota(jnp.int32, (block_rows, hd), 1).astype(jnp.float32)
        picks = [jnp.where(pos - i * hd == lanes, 1.0, 0.0) for i in range(group // hd)]
        pick = jnp.concatenate([p.astype(jnp.bfloat16) for p in picks], axis=1)
        query = jnp.dot(pick, kv[0, :, 0:hd], preferred_element_type=jnp.float32)
        query = query.astype(jnp.bfloat16)
        highest = None
        for part in range(3):
            score = lax.dot_general(
                query,
                kv[part, :, hd : 2 * hd],
                (((1,), (1,)), ((), ())),
                preferred_element_type=jnp.float32,
            )
            scores[part] = score
            top = jnp.max(score, axis=-1, keepdims=True)
            highest = top if highest is None else jnp.maximum(highest, top)
        total = jnp.zeros((block_rows, 2 * hd), jnp.float32)
        for part in range(3):
            weights = jnp.exp2((scores[part] - highest) * factor).astype(jnp.bfloat16)
            total += jnp.dot(weights, kv[part, :, 2 * hd :], preferred_element_type=jnp.float32)
        result = (total[:, :hd] / total[:, hd:]).astype(jnp.bfloat16)

        @pl.when(zz == z)
        def _():
            attn_in[z] = result

        @pl.when(zz != z)
        def _():
            attn[zz] = result
            attn_copy(zz).start()

        return carry

    lax.fori_loop(0, n_z, attend_block, 0)

    def weights_in(zz):
        for k in range(1, n_tm):
            w_peer(k, zz, (tm + n_tm - k) % n_tm).wait_recv()

    others(weights_in)
    others(lambda zz: attn_arrival(zz).wait_recv())

    def heads(side):
        rows = rows_of(side, tokens)
        return jnp.concatenate([attn_in[zz, rows, :] for zz in range(n_z)], axis=1)

    left = jnp.concatenate([heads(1 - core), heads(core)], axis=0)
    for j in range(n_tm):
        both = jnp.dot(left, wall[j], preferred_element_type=jnp.float32)
        part_out[j] = both[:tokens].astype(jnp.bfloat16)
        part_copy(j).start()
        own[j] = both[tokens:]
    for j in range(n_tm):
        part_copy(j).wait_recv()
        total = own[j] + part_in[j].astype(jnp.float32)
        out_ref[:, j * quarter : (j + 1) * quarter] = total.astype(jnp.bfloat16)

    for j in range(n_tm):
        part_copy(j).wait_send()

    def sent(zz):
        attn_copy(zz).wait_send()
        for k in range(1, n_tm):
            w_peer(k, zz, tm).wait_send()

    others(sent)

    for zz in range(n_z):

        @pl.when(tm > 0)
        def _():
            kv_copy(0, zz).wait_send()

        @pl.when(tm < n_tm - 1)
        def _():
            kv_copy(1, zz).wait_send()

        far = jnp.logical_and(outer, zz == n_z - 1 - z)

        @pl.when(jnp.logical_not(far))
        def _():
            x_sibling(zz, core).wait_send()

    for u in range(n_z - 1):
        for way in (0, 1):
            zz = z - u if way == 0 else z + u

            @pl.when(jnp.logical_and(inside(zz), forwards_w(way)))
            def _():
                w_ring(way, u, zz).wait_send()

            for part in (0, 1):
                live = u < n_z - 2
                if u == 0 and part == 0:
                    live = inner

                @pl.when(jnp.logical_and(jnp.logical_and(live, inside(zz)), forwards_w(way)))
                def _():
                    x_ring(way, u, zz, part).wait_send()

    @pl.when(inner)
    def _():
        wq_peer(0, tm).wait_send()
        wq_peer(1, tm).wait_send()
        wq_peer(2, beside).wait_send()
        qkv_outward(n_z - 1 - end_of).wait_send()


def fused(n_tm, n_z, frame, x, wq, wo, q_gain, k_gain, perm):
    tokens, model = x.shape
    hd = wo.shape[0]
    shards = 2 * n_z
    group = shards * tokens
    bf = jnp.bfloat16
    dma = pltpu.SemaphoreType.DMA
    vmem = pl.BlockSpec(memory_space=pltpu.VMEM)
    return pl.pallas_call(
        functools.partial(fused_kernel, n_tm, n_z, frame),
        out_shape=jax.ShapeDtypeStruct((tokens, model), bf),
        in_specs=[vmem] * 6,
        out_specs=vmem,
        scratch_shapes=[
            pltpu.VMEM((shards, tokens, model), bf),
            pltpu.VMEM((n_tm, n_z * hd, model // n_tm), bf),
            pltpu.VMEM((model, 3 * hd), bf),
            pltpu.VMEM((2 * tokens, 3 * hd), bf),
            pltpu.VMEM((group, hd), jnp.float32),
            pltpu.VMEM((3, group, 4 * hd), bf),
            pltpu.VMEM((3, 2 * tokens, group), jnp.float32),
            pltpu.VMEM((n_z, 2 * tokens, hd), bf),
            pltpu.VMEM((n_z, 2 * tokens, hd), bf),
            pltpu.VMEM((n_tm, tokens, model // n_tm), bf),
            pltpu.VMEM((n_tm, tokens, model // n_tm), bf),
            pltpu.VMEM((n_tm, tokens, model // n_tm), jnp.float32),
            dma((2, n_z)),
            dma((2, n_z)),
            dma((n_tm - 1, n_z)),
            dma((n_tm - 1, n_z)),
            dma((2, n_z, 2)),
            dma((2, n_z, 2)),
            dma((n_z,)),
            dma((n_z,)),
            dma((2, n_z)),
            dma((2, n_z)),
            dma((n_z,)),
            dma((n_z,)),
            dma((n_tm,)),
            dma((n_tm,)),
            dma,
            dma,
            dma((n_tm - 1,)),
            dma((n_tm - 1,)),
            dma,
            dma,
        ],
        compiler_params=pltpu.CompilerParams(
            collective_id=0, has_side_effects=True, vmem_limit_bytes=56 * 1024 * 1024
        ),
    )(x, wq, wo, q_gain, k_gain, perm)


def whole_window(video, w_qkv, w_out, q_gain, k_gain, tile_perm):
    frames, rows_here, cols, model = video.shape
    n_tm = lax.axis_size("tm")
    n_space = lax.axis_size("space")
    hd = w_out.shape[1]
    tokens = frames * rows_here * cols
    mixed = fused(
        n_tm,
        n_space // 2,
        (rows_here, cols, rows_here * n_space * cols),
        video.reshape(tokens, model),
        w_qkv.reshape(model, 3 * hd),
        w_out.reshape(hd, model),
        q_gain.reshape(1, hd),
        k_gain.reshape(1, hd),
        tile_perm,
    )
    return mixed[None]


def extended(cells, sides, width):
    for axis, dim in sides:
        count = lax.axis_size(axis)
        ends = count - 1
        head = lax.slice_in_dim(cells, 0, width, axis=dim)
        tail = lax.slice_in_dim(cells, cells.shape[dim] - width, cells.shape[dim], axis=dim)
        cells = jnp.concatenate(
            [
                lax.ppermute(tail, axis, [(i, (i + 1) % count) for i in range(ends)]),
                cells,
                lax.ppermute(head, axis, [((i + 1) % count, i) for i in range(ends)]),
            ],
            axis=dim,
        )
    return cells


def head_norm(values, gain):
    wide = values.astype(jnp.float32)
    scaled = wide * lax.rsqrt(jnp.mean(wide * wide, axis=-1, keepdims=True) + 1e-06)
    return (scaled * gain).astype(jnp.bfloat16)


def attend(queries, chosen, valid):
    heads_here = queries.shape[1]
    head_dim = queries.shape[2]
    span = chosen.shape[1] * chosen.shape[2]
    keys = chosen[:, :, :, :, 0, :].reshape(-1, heads_here, head_dim)
    values = chosen[:, :, :, :, 1, :].reshape(-1, heads_here, head_dim)
    scores = jnp.einsum(
        "qhd,khd->hqk", queries, keys, preferred_element_type=jnp.float32
    ) * head_dim ** (-0.5)
    live = jnp.repeat(valid, span)
    scores = jnp.where(live[None, None, :], scores, -jnp.inf)
    highest = jnp.max(scores, axis=-1, keepdims=True)
    weights = jnp.exp(scores - highest)
    probs = (weights / jnp.sum(weights, axis=-1, keepdims=True)).astype(jnp.bfloat16)
    result = jnp.einsum("hqk,khd->qhd", probs, values, preferred_element_type=jnp.float32)
    return result.astype(jnp.bfloat16)


def per_device(video, w_qkv, w_out, q_gain, k_gain, tile_perm, window):
    tiles = video.shape[0] * video.shape[1] * lax.axis_size("space") * video.shape[2] // (TT * TH * TW)
    sized = lax.axis_size("tm") == 4 and lax.axis_size("space") == 8
    if window.shape[1] == tiles and w_qkv.shape[1] == 1 and sized:
        return whole_window(video, w_qkv, w_out, q_gain, k_gain, tile_perm)
    frames_here = video.shape[0]
    cols_here = video.shape[2]
    model_dim = video.shape[3]
    heads_here = w_qkv.shape[1]
    head_dim = w_out.shape[1]
    flat_w = w_qkv.reshape(model_dim, heads_here * 3 * head_dim)
    qkv = jnp.einsum(
        "frwd,dc->frwc",
        lax.all_gather(video, "space", axis=1, tiled=True),
        flat_w,
        preferred_element_type=jnp.float32,
    ).astype(jnp.bfloat16)
    group_tokens = frames_here * qkv.shape[1] * cols_here
    qkv = qkv.reshape(group_tokens, heads_here, 3, head_dim)
    ordered = jnp.take(qkv, tile_perm[0], axis=0)
    queries = head_norm(ordered[:, :, 0, :], q_gain)
    keys = head_norm(ordered[:, :, 1, :], k_gain)
    pairs = jnp.stack([keys, ordered[:, :, 2, :]], axis=2)
    beside_all = extended(pairs[None], (("tm", 0),), 1)
    tile_tokens = TT * TH * TW
    tile_count = group_tokens // tile_tokens
    beside_all = beside_all.reshape(3, tile_count, tile_tokens, heads_here, 2, head_dim)
    position = lax.axis_index("tm")
    valid = jnp.stack([position > 0, position >= 0, position < lax.axis_size("tm") - 1])
    query_tiles = queries.reshape(tile_count, tile_tokens, heads_here, head_dim)

    def one_tile(item):
        block, picks = item
        return attend(block, jnp.take(beside_all, picks, axis=1), valid)

    attn = lax.map(one_tile, (query_tiles, window)).reshape(group_tokens, heads_here, head_dim)
    flat_attn = attn.reshape(group_tokens, heads_here * head_dim)
    flat_out = w_out.reshape(heads_here * head_dim, model_dim)
    product = jnp.dot(flat_attn, flat_out, preferred_element_type=jnp.float32)
    summed = lax.psum_scatter(
        lax.optimization_barrier(product.astype(jnp.bfloat16))
        .astype(jnp.float32)
        .astype(jnp.bfloat16),
        "space",
        scatter_dimension=0,
        tiled=True,
    )
    return summed[None]


def solution(mesh):
    in_specs = (
        P("tm", "space", None, None),
        P(None, "space", None),
        P("space", None, None),
        P(),
        P(),
        P("tm", None),
        P(),
    )
    out_specs = P("tm", "space", None)
    return jax.shard_map(
        per_device, mesh=mesh, in_specs=in_specs, out_specs=out_specs, check_vma=False
    )
```

```python
import functools
import math

import jax
import jax.numpy as jnp
from jax import lax
from jax.experimental import pallas as pl
from jax.experimental.pallas import tpu as pltpu
from jax.sharding import PartitionSpec as P

MESH = pl.DeviceIdType.MESH
TT = 4
TH = 8
TW = 8


def fused_kernel(
    n_tm,
    n_z,
    frame,
    x_ref,
    wq_ref,
    wo_ref,
    qg_ref,
    kg_ref,
    perm_ref,
    out_ref,
    xg,
    wall,
    inner_w,
    stage,
    place,
    kv,
    scores,
    attn,
    attn_in,
    part_out,
    part_in,
    own,
    wz_send,
    wz_recv,
    wt_send,
    wt_recv,
    x_send,
    x_recv,
    sib_send,
    sib_recv,
    kv_send,
    kv_recv,
    at_send,
    at_recv,
    pt_send,
    pt_recv,
    wq_send,
    wq_recv,
    wp_send,
    wp_recv,
    qkv_send,
    qkv_recv,
):
    tm = lax.axis_index("tm")
    space = lax.axis_index("space")
    z = space // 2
    core = space % 2
    sibling = z * 2 + 1 - core
    tokens, model = x_ref.shape
    shards = 2 * n_z
    group = shards * tokens
    hd = kv.shape[2] // 4
    quarter = model // n_tm
    inner = jnp.logical_and(z > 0, z < n_z - 1)
    outer = jnp.logical_not(inner)
    end_of = (z - 1) * (n_z - 1)
    inner_of = 1 + z // (n_z - 1)

    def remote(src, dst, send, recv, t, s):
        return pltpu.make_async_remote_copy(
            src_ref=src, dst_ref=dst, send_sem=send, recv_sem=recv,
            device_id=(t, s), device_id_type=MESH,
        )

    def rows_of(index, count):
        return pl.ds(pl.multiple_of(index * count, count), count)

    def w_ring(way, u, zz):
        target = z + 1 if way == 0 else z - 1
        block = wall.at[tm, rows_of(zz, hd)]
        return remote(block, block, wz_send.at[way, u], wz_recv.at[way, u], tm, target * 2 + core)

    def x_ring(way, u, zz, part):
        target = z + 1 if way == 0 else z - 1
        block = xg.at[zz * 2 + core, pl.ds(part * (tokens // 2), tokens // 2)]
        return remote(
            block, block, x_send.at[way, u, part], x_recv.at[way, u, part], tm, target * 2 + core
        )

    def w_peer(k, zz, owner):
        block = wall.at[owner, rows_of(zz, hd)]
        return remote(
            block, block, wt_send.at[k - 1, zz], wt_recv.at[k - 1, zz], (tm + k) % n_tm, space
        )

    def x_sibling(zz, side, part):
        block = xg.at[zz * 2 + side, pl.ds(part * (tokens // 2), tokens // 2)]
        return remote(block, block, sib_send.at[zz, part], sib_recv.at[zz, part], tm, sibling)

    def kv_copy(way, zz, side):
        target = tm - 1 if way == 0 else tm + 1
        rows = rows_of(zz * 2 + side, tokens)
        return remote(
            kv.at[0, rows, pl.ds(hd, 2 * hd)],
            kv.at[2 - way, rows, pl.ds(hd, 2 * hd)],
            kv_send.at[way, zz, side],
            kv_recv.at[way, zz, side],
            target,
            space,
        )

    def wq_inward():
        rows = rows_of(tm, quarter)
        return remote(
            wq_ref.at[rows], inner_w.at[rows], wq_send, wq_recv, tm, inner_of * 2 + core
        )

    beside = tm + 1 - 2 * (tm % 2)
    across = (tm + n_tm // 2) % n_tm

    def wq_peer(k, owner):
        block = inner_w.at[rows_of(owner, quarter)]
        target = beside if k == 0 else across
        return remote(block, block, wp_send.at[k], wp_recv.at[k], target, space)

    def qkv_outward(zz, turn):
        side = core + turn * (1 - 2 * core)
        return remote(
            stage.at[turn],
            kv.at[0, rows_of(zz * 2 + side, tokens), pl.ds(0, 3 * hd)],
            qkv_send.at[turn],
            qkv_recv.at[turn],
            tm,
            end_of * 2 + core,
        )

    def attn_copy(zz):
        return remote(
            attn.at[zz], attn_in.at[z], at_send.at[zz], at_recv.at[z], tm, zz * 2 + core
        )

    def attn_arrival(zz):
        return remote(
            attn.at[zz], attn_in.at[zz], at_send.at[zz], at_recv.at[zz], tm, zz * 2 + core
        )

    def part_copy(j):
        return remote(
            part_out.at[j], part_in.at[j], pt_send.at[j], pt_recv.at[j], tm, sibling
        )

    barrier = pltpu.get_barrier_semaphore()
    for k in range(1, n_z):
        pl.semaphore_signal(
            barrier, inc=1, device_id=(tm, (z + k) % n_z * 2 + core), device_id_type=MESH
        )
    for k in range(1, n_tm):
        pl.semaphore_signal(barrier, inc=1, device_id=((tm + k) % n_tm, space), device_id_type=MESH)
    pl.semaphore_signal(barrier, inc=1, device_id=(tm, sibling), device_id_type=MESH)
    for j in range(n_tm):
        wall[j, rows_of(z, hd), :] = wo_ref[:, j * quarter : (j + 1) * quarter]
    xg[space] = x_ref[...]
    kv[0, :, 3 * hd :] = jnp.ones((group, hd), jnp.bfloat16)
    pl.semaphore_wait(barrier, n_z - 1 + n_tm - 1 + 1)

    def norm(value, gain):
        scaled = value * lax.rsqrt(jnp.mean(value * value, axis=-1, keepdims=True) + 1e-06)
        return (scaled * gain).astype(jnp.bfloat16)

    def project(x, weights):
        qkv = jnp.dot(x, weights[...], preferred_element_type=jnp.float32)
        qkv = qkv.astype(jnp.bfloat16)
        query = norm(qkv[:, :hd].astype(jnp.float32), qg_ref[...])
        key = norm(qkv[:, hd : 2 * hd].astype(jnp.float32), kg_ref[...])
        return jnp.concatenate([query, key, qkv[:, 2 * hd :]], axis=1)

    def inside(zz):
        return jnp.logical_and(zz >= 0, zz < n_z)

    def forwards_w(way):
        return z < n_z - 1 if way == 0 else z > 0

    def spread_w(u):
        for way in (0, 1):
            zz = z - u if way == 0 else z + u
            live = inside(zz)

            @pl.when(jnp.logical_and(live, u > 0))
            def _():
                w_ring(way, u - 1, zz).wait_recv()

            @pl.when(jnp.logical_and(live, forwards_w(way)))
            def _():
                w_ring(way, u, zz).start()

            @pl.when(jnp.logical_and(jnp.logical_and(live, outer), u > 0))
            def _():
                for k in range(1, n_tm):
                    w_peer(k, zz, tm).start()

    def step(u, carry):
        def arrive(part):
            for way in (0, 1):
                zz = z - u if way == 0 else z + u

                @pl.when(jnp.logical_and(inside(zz), jnp.logical_and(u > 0, u < n_z - 1)))
                def _():
                    x_ring(way, u - 1, zz, part).wait_recv()

                going = jnp.logical_and(jnp.logical_or(inner, u >= part), u < n_z - 2)

                @pl.when(jnp.logical_and(jnp.logical_and(inside(zz), going), forwards_w(way)))
                def _():
                    x_ring(way, u, zz, part).start()

                live = jnp.logical_and(inside(zz), u < n_z - 1)
                fresh = live if way == 0 else jnp.logical_and(live, u > 0)

                @pl.when(fresh)
                def _():
                    x_sibling(zz, core, part).start()

        arrive(0)

        @pl.when(jnp.logical_and(inner, u == 1))
        def _():
            wq_inward().wait_recv()
            for k in (0, 1):
                wq_peer(k, tm).start()

        arrive(1)

        @pl.when(jnp.logical_and(inner, u == 1))
        def _():
            wq_peer(0, beside).wait_recv()
            wq_peer(2, beside).start()

        last = jnp.logical_and(inner, u == n_z - 2)

        @pl.when(last)
        def _():
            wq_peer(1, across).wait_recv()
            wq_peer(2, (beside + n_tm // 2) % n_tm).wait_recv()
            far = n_z - 1 - end_of

            def send(turn, carry):
                @pl.when(turn == 1)
                def _():
                    for part in (0, 1):
                        x_sibling(far, 1 - core, part).wait_recv()

                slot = far * 2 + core + turn * (1 - 2 * core)
                stage[turn] = project(xg[slot], inner_w)
                qkv_outward(far, turn).start()
                return carry

            lax.fori_loop(0, 2, send, 0)

        @pl.when(outer)
        def _():
            spread_w(u)

        def item(way, carry):
            zz = z - u + way * 2 * u
            fresh = jnp.logical_and(inside(zz), way * (1 - jnp.minimum(u, 1)) == 0)

            @pl.when(jnp.logical_and(fresh, u < n_z - 1))
            def _():
                @pl.when(jnp.logical_not(last))
                def _():
                    for part in (0, 1):
                        x_sibling(zz, 1 - core, part).wait_recv()

                both = xg[rows_of(zz, 2)].reshape(2 * tokens, model)
                kv[0, rows_of(zz, 2 * tokens), 0 : 3 * hd] = project(both, wq_ref)

            for turn in (0, 1):
                side = core + turn * (1 - 2 * core)

                @pl.when(jnp.logical_and(fresh, u == n_z - 1))
                def _():
                    qkv_outward(zz, turn).wait_recv()

                @pl.when(jnp.logical_and(fresh, tm > 0))
                def _():
                    kv_copy(0, zz, side).start()

                @pl.when(jnp.logical_and(fresh, tm < n_tm - 1))
                def _():
                    kv_copy(1, zz, side).start()

            return carry

        lax.fori_loop(0, 2, item, 0)

        for way in (0, 1):

            @pl.when(jnp.logical_and(jnp.logical_and(outer, u == 0), forwards_w(way)))
            def _():
                x_ring(way, u, z, 0).wait_send()
                wq_inward().start()
                wq_inward().wait_send()
                x_ring(way, u, z, 1).start()

        @pl.when(inner)
        def _():
            spread_w(u)

        return carry

    token = perm_ref[...].astype(jnp.float32)
    rows_here, cols, plane = frame

    def whole(value, by):
        return jnp.floor((value + 0.5) * (1.0 / by))

    at_frame = whole(token, plane)
    token = token - at_frame * plane
    row = whole(token, cols)
    col = token - row * cols
    shard = whole(row, rows_here)
    pos = shard * tokens + (at_frame * rows_here + row - shard * rows_here) * cols + col
    for i in range(group // hd):
        block = jnp.broadcast_to(pos[:, i * hd : (i + 1) * hd], (hd, hd))
        place[i * hd : (i + 1) * hd, :] = block.T

    lax.fori_loop(0, n_z, step, 0)

    def others(body):
        for k in range(1, n_z):
            body((z + k) % n_z)

    def weights_out(zz):
        for k in range(1, n_tm):
            w_peer(k, zz, tm).start()

    @pl.when(inner)
    def _():
        others(weights_out)

    for way in (0, 1):
        here = 2 - way
        live = tm < n_tm - 1 if way == 0 else tm > 0

        @pl.when(live)
        def _():
            kv[here, :, 3 * hd :] = jnp.ones((group, hd), jnp.bfloat16)

            for zz in range(n_z):
                for side in (0, 1):
                    kv_copy(way, zz, side).wait_recv()

        @pl.when(jnp.logical_not(live))
        def _():
            kv[here, :, hd : 2 * hd] = kv[0, :, hd : 2 * hd]
            kv[here, :, 2 * hd :] = jnp.zeros((group, 2 * hd), jnp.bfloat16)

    factor = math.log2(math.e) * hd**-0.5
    block_rows = 2 * tokens

    def attend_block(i, carry):
        zz = (z + 1 + i) % n_z
        pos = place[rows_of(zz, block_rows), :]
        lanes = lax.broadcasted_iota(jnp.int32, (block_rows, hd), 1).astype(jnp.float32)
        picks = [jnp.where(pos - i * hd == lanes, 1.0, 0.0) for i in range(group // hd)]
        pick = jnp.concatenate([p.astype(jnp.bfloat16) for p in picks], axis=1)
        query = jnp.dot(pick, kv[0, :, 0:hd], preferred_element_type=jnp.float32)
        query = query.astype(jnp.bfloat16)
        highest = None
        for part in range(3):
            score = lax.dot_general(
                query,
                kv[part, :, hd : 2 * hd],
                (((1,), (1,)), ((), ())),
                preferred_element_type=jnp.float32,
            )
            scores[part] = score
            top = jnp.max(score, axis=-1, keepdims=True)
            highest = top if highest is None else jnp.maximum(highest, top)
        total = jnp.zeros((block_rows, 2 * hd), jnp.float32)
        for part in range(3):
            weights = jnp.exp2((scores[part] - highest) * factor).astype(jnp.bfloat16)
            total += jnp.dot(weights, kv[part, :, 2 * hd :], preferred_element_type=jnp.float32)
        result = (total[:, :hd] / total[:, hd:]).astype(jnp.bfloat16)

        @pl.when(zz == z)
        def _():
            attn_in[z] = result

        @pl.when(zz != z)
        def _():
            attn[zz] = result
            attn_copy(zz).start()

        return carry

    lax.fori_loop(0, n_z, attend_block, 0)

    def weights_in(zz):
        for k in range(1, n_tm):
            w_peer(k, zz, (tm + n_tm - k) % n_tm).wait_recv()

    others(weights_in)
    others(lambda zz: attn_arrival(zz).wait_recv())

    def heads(side):
        rows = rows_of(side, tokens)
        return jnp.concatenate([attn_in[zz, rows, :] for zz in range(n_z)], axis=1)

    left = jnp.concatenate([heads(1 - core), heads(core)], axis=0)
    for j in range(n_tm):
        both = jnp.dot(left, wall[j], preferred_element_type=jnp.float32)
        part_out[j] = both[:tokens].astype(jnp.bfloat16)
        part_copy(j).start()
        own[j] = both[tokens:]
    for j in range(n_tm):
        part_copy(j).wait_recv()
        total = own[j] + part_in[j].astype(jnp.float32)
        out_ref[:, j * quarter : (j + 1) * quarter] = total.astype(jnp.bfloat16)

    for j in range(n_tm):
        part_copy(j).wait_send()

    def sent(zz):
        attn_copy(zz).wait_send()
        for k in range(1, n_tm):
            w_peer(k, zz, tm).wait_send()

    others(sent)

    for zz in range(n_z):

        @pl.when(tm > 0)
        def _():
            for side in (0, 1):
                kv_copy(0, zz, side).wait_send()

        @pl.when(tm < n_tm - 1)
        def _():
            for side in (0, 1):
                kv_copy(1, zz, side).wait_send()

        far = jnp.logical_and(outer, zz == n_z - 1 - z)

        @pl.when(jnp.logical_not(far))
        def _():
            for part in (0, 1):
                x_sibling(zz, core, part).wait_send()

    for u in range(n_z - 1):
        for way in (0, 1):
            zz = z - u if way == 0 else z + u

            @pl.when(jnp.logical_and(inside(zz), forwards_w(way)))
            def _():
                w_ring(way, u, zz).wait_send()

            for part in (0, 1):
                live = u < n_z - 2
                if u == 0 and part == 0:
                    live = inner

                @pl.when(jnp.logical_and(jnp.logical_and(live, inside(zz)), forwards_w(way)))
                def _():
                    x_ring(way, u, zz, part).wait_send()

    @pl.when(inner)
    def _():
        wq_peer(0, tm).wait_send()
        wq_peer(1, tm).wait_send()
        wq_peer(2, beside).wait_send()
        for turn in (0, 1):
            qkv_outward(n_z - 1 - end_of, turn).wait_send()


def fused(n_tm, n_z, frame, x, wq, wo, q_gain, k_gain, perm):
    tokens, model = x.shape
    hd = wo.shape[0]
    shards = 2 * n_z
    group = shards * tokens
    bf = jnp.bfloat16
    dma = pltpu.SemaphoreType.DMA
    vmem = pl.BlockSpec(memory_space=pltpu.VMEM)
    return pl.pallas_call(
        functools.partial(fused_kernel, n_tm, n_z, frame),
        out_shape=jax.ShapeDtypeStruct((tokens, model), bf),
        in_specs=[vmem] * 6,
        out_specs=vmem,
        scratch_shapes=[
            pltpu.VMEM((shards, tokens, model), bf),
            pltpu.VMEM((n_tm, n_z * hd, model // n_tm), bf),
            pltpu.VMEM((model, 3 * hd), bf),
            pltpu.VMEM((2, tokens, 3 * hd), bf),
            pltpu.VMEM((group, hd), jnp.float32),
            pltpu.VMEM((3, group, 4 * hd), bf),
            pltpu.VMEM((3, 2 * tokens, group), jnp.float32),
            pltpu.VMEM((n_z, 2 * tokens, hd), bf),
            pltpu.VMEM((n_z, 2 * tokens, hd), bf),
            pltpu.VMEM((n_tm, tokens, model // n_tm), bf),
            pltpu.VMEM((n_tm, tokens, model // n_tm), bf),
            pltpu.VMEM((n_tm, tokens, model // n_tm), jnp.float32),
            dma((2, n_z)),
            dma((2, n_z)),
            dma((n_tm - 1, n_z)),
            dma((n_tm - 1, n_z)),
            dma((2, n_z, 2)),
            dma((2, n_z, 2)),
            dma((n_z, 2)),
            dma((n_z, 2)),
            dma((2, n_z, 2)),
            dma((2, n_z, 2)),
            dma((n_z,)),
            dma((n_z,)),
            dma((n_tm,)),
            dma((n_tm,)),
            dma,
            dma,
            dma((n_tm - 1,)),
            dma((n_tm - 1,)),
            dma((2,)),
            dma((2,)),
        ],
        compiler_params=pltpu.CompilerParams(
            collective_id=0, has_side_effects=True, vmem_limit_bytes=56 * 1024 * 1024
        ),
    )(x, wq, wo, q_gain, k_gain, perm)


def whole_window(video, w_qkv, w_out, q_gain, k_gain, tile_perm):
    frames, rows_here, cols, model = video.shape
    n_tm = lax.axis_size("tm")
    n_space = lax.axis_size("space")
    hd = w_out.shape[1]
    tokens = frames * rows_here * cols
    mixed = fused(
        n_tm,
        n_space // 2,
        (rows_here, cols, rows_here * n_space * cols),
        video.reshape(tokens, model),
        w_qkv.reshape(model, 3 * hd),
        w_out.reshape(hd, model),
        q_gain.reshape(1, hd),
        k_gain.reshape(1, hd),
        tile_perm,
    )
    return mixed[None]


def extended(cells, sides, width):
    for axis, dim in sides:
        count = lax.axis_size(axis)
        ends = count - 1
        head = lax.slice_in_dim(cells, 0, width, axis=dim)
        tail = lax.slice_in_dim(cells, cells.shape[dim] - width, cells.shape[dim], axis=dim)
        cells = jnp.concatenate(
            [
                lax.ppermute(tail, axis, [(i, (i + 1) % count) for i in range(ends)]),
                cells,
                lax.ppermute(head, axis, [((i + 1) % count, i) for i in range(ends)]),
            ],
            axis=dim,
        )
    return cells


def head_norm(values, gain):
    wide = values.astype(jnp.float32)
    scaled = wide * lax.rsqrt(jnp.mean(wide * wide, axis=-1, keepdims=True) + 1e-06)
    return (scaled * gain).astype(jnp.bfloat16)


def attend(queries, chosen, valid):
    heads_here = queries.shape[1]
    head_dim = queries.shape[2]
    span = chosen.shape[1] * chosen.shape[2]
    keys = chosen[:, :, :, :, 0, :].reshape(-1, heads_here, head_dim)
    values = chosen[:, :, :, :, 1, :].reshape(-1, heads_here, head_dim)
    scores = jnp.einsum(
        "qhd,khd->hqk", queries, keys, preferred_element_type=jnp.float32
    ) * head_dim ** (-0.5)
    live = jnp.repeat(valid, span)
    scores = jnp.where(live[None, None, :], scores, -jnp.inf)
    highest = jnp.max(scores, axis=-1, keepdims=True)
    weights = jnp.exp(scores - highest)
    probs = (weights / jnp.sum(weights, axis=-1, keepdims=True)).astype(jnp.bfloat16)
    result = jnp.einsum("hqk,khd->qhd", probs, values, preferred_element_type=jnp.float32)
    return result.astype(jnp.bfloat16)


def per_device(video, w_qkv, w_out, q_gain, k_gain, tile_perm, window):
    tiles = video.shape[0] * video.shape[1] * lax.axis_size("space") * video.shape[2] // (TT * TH * TW)
    sized = lax.axis_size("tm") == 4 and lax.axis_size("space") == 8
    if window.shape[1] == tiles and w_qkv.shape[1] == 1 and sized:
        return whole_window(video, w_qkv, w_out, q_gain, k_gain, tile_perm)
    frames_here = video.shape[0]
    cols_here = video.shape[2]
    model_dim = video.shape[3]
    heads_here = w_qkv.shape[1]
    head_dim = w_out.shape[1]
    flat_w = w_qkv.reshape(model_dim, heads_here * 3 * head_dim)
    qkv = jnp.einsum(
        "frwd,dc->frwc",
        lax.all_gather(video, "space", axis=1, tiled=True),
        flat_w,
        preferred_element_type=jnp.float32,
    ).astype(jnp.bfloat16)
    group_tokens = frames_here * qkv.shape[1] * cols_here
    qkv = qkv.reshape(group_tokens, heads_here, 3, head_dim)
    ordered = jnp.take(qkv, tile_perm[0], axis=0)
    queries = head_norm(ordered[:, :, 0, :], q_gain)
    keys = head_norm(ordered[:, :, 1, :], k_gain)
    pairs = jnp.stack([keys, ordered[:, :, 2, :]], axis=2)
    beside_all = extended(pairs[None], (("tm", 0),), 1)
    tile_tokens = TT * TH * TW
    tile_count = group_tokens // tile_tokens
    beside_all = beside_all.reshape(3, tile_count, tile_tokens, heads_here, 2, head_dim)
    position = lax.axis_index("tm")
    valid = jnp.stack([position > 0, position >= 0, position < lax.axis_size("tm") - 1])
    query_tiles = queries.reshape(tile_count, tile_tokens, heads_here, head_dim)

    def one_tile(item):
        block, picks = item
        return attend(block, jnp.take(beside_all, picks, axis=1), valid)

    attn = lax.map(one_tile, (query_tiles, window)).reshape(group_tokens, heads_here, head_dim)
    flat_attn = attn.reshape(group_tokens, heads_here * head_dim)
    flat_out = w_out.reshape(heads_here * head_dim, model_dim)
    product = jnp.dot(flat_attn, flat_out, preferred_element_type=jnp.float32)
    summed = lax.psum_scatter(
        lax.optimization_barrier(product.astype(jnp.bfloat16))
        .astype(jnp.float32)
        .astype(jnp.bfloat16),
        "space",
        scatter_dimension=0,
        tiled=True,
    )
    return summed[None]


def solution(mesh):
    in_specs = (
        P("tm", "space", None, None),
        P(None, "space", None),
        P("space", None, None),
        P(),
        P(),
        P("tm", None),
        P(),
    )
    out_specs = P("tm", "space", None)
    return jax.shard_map(
        per_device, mesh=mesh, in_specs=in_specs, out_specs=out_specs, check_vma=False
    )
```

```python
import functools
import math

import jax
import jax.numpy as jnp
from jax import lax
from jax.experimental import pallas as pl
from jax.experimental.pallas import tpu as pltpu
from jax.sharding import PartitionSpec as P

MESH = pl.DeviceIdType.MESH
TT = 4
TH = 8
TW = 8


def fused_kernel(
    n_tm,
    n_z,
    frame,
    x_ref,
    wq_ref,
    wo_ref,
    qg_ref,
    kg_ref,
    perm_ref,
    out_ref,
    xg,
    wall,
    inner_w,
    stage,
    place,
    kv,
    scores,
    attn,
    attn_in,
    part_out,
    part_in,
    own,
    wz_send,
    wz_recv,
    wt_send,
    wt_recv,
    x_send,
    x_recv,
    sib_send,
    sib_recv,
    kv_send,
    kv_recv,
    at_send,
    at_recv,
    pt_send,
    pt_recv,
    wq_send,
    wq_recv,
    wp_send,
    wp_recv,
    qkv_send,
    qkv_recv,
):
    tm = lax.axis_index("tm")
    space = lax.axis_index("space")
    z = space // 2
    core = space % 2
    sibling = z * 2 + 1 - core
    tokens, model = x_ref.shape
    shards = 2 * n_z
    group = shards * tokens
    hd = kv.shape[2] // 4
    quarter = model // n_tm
    inner = jnp.logical_and(z > 0, z < n_z - 1)
    outer = jnp.logical_not(inner)
    end_of = (z - 1) * (n_z - 1)
    inner_of = 1 + z // (n_z - 1)

    def remote(src, dst, send, recv, t, s):
        return pltpu.make_async_remote_copy(
            src_ref=src, dst_ref=dst, send_sem=send, recv_sem=recv,
            device_id=(t, s), device_id_type=MESH,
        )

    def rows_of(index, count):
        return pl.ds(pl.multiple_of(index * count, count), count)

    def w_ring(way, u, zz):
        target = z + 1 if way == 0 else z - 1
        block = wall.at[tm, rows_of(zz, hd)]
        return remote(block, block, wz_send.at[way, u], wz_recv.at[way, u], tm, target * 2 + core)

    def x_ring(way, u, zz, part):
        target = z + 1 if way == 0 else z - 1
        block = xg.at[zz * 2 + core, pl.ds(part * (tokens // 2), tokens // 2)]
        return remote(
            block, block, x_send.at[way, u, part], x_recv.at[way, u, part], tm, target * 2 + core
        )

    def w_peer(k, zz, owner):
        block = wall.at[owner, rows_of(zz, hd)]
        return remote(
            block, block, wt_send.at[k - 1, zz], wt_recv.at[k - 1, zz], (tm + k) % n_tm, space
        )

    def x_sibling(zz, side, part):
        block = xg.at[zz * 2 + side, pl.ds(part * (tokens // 2), tokens // 2)]
        return remote(block, block, sib_send.at[zz, part], sib_recv.at[zz, part], tm, sibling)

    def kv_copy(way, zz, side):
        target = tm - 1 if way == 0 else tm + 1
        rows = rows_of(zz * 2 + side, tokens)
        return remote(
            kv.at[0, rows, pl.ds(hd, 2 * hd)],
            kv.at[2 - way, rows, pl.ds(hd, 2 * hd)],
            kv_send.at[way, zz, side],
            kv_recv.at[way, zz, side],
            target,
            space,
        )

    def wq_inward():
        rows = rows_of(tm, quarter)
        return remote(
            wq_ref.at[rows], inner_w.at[rows], wq_send, wq_recv, tm, inner_of * 2 + core
        )

    beside = tm + 1 - 2 * (tm % 2)
    across = (tm + n_tm // 2) % n_tm

    def wq_peer(k, owner):
        block = inner_w.at[rows_of(owner, quarter)]
        target = beside if k == 0 else across
        return remote(block, block, wp_send.at[k], wp_recv.at[k], target, space)

    def qkv_outward(zz, turn):
        side = core + turn * (1 - 2 * core)
        return remote(
            stage.at[turn],
            kv.at[0, rows_of(zz * 2 + side, tokens), pl.ds(0, 3 * hd)],
            qkv_send.at[turn],
            qkv_recv.at[turn],
            tm,
            end_of * 2 + core,
        )

    def attn_copy(zz):
        return remote(
            attn.at[zz], attn_in.at[z], at_send.at[zz], at_recv.at[z], tm, zz * 2 + core
        )

    def attn_arrival(zz):
        return remote(
            attn.at[zz], attn_in.at[zz], at_send.at[zz], at_recv.at[zz], tm, zz * 2 + core
        )

    def part_copy(j):
        return remote(
            part_out.at[j], part_in.at[j], pt_send.at[j], pt_recv.at[j], tm, sibling
        )

    barrier = pltpu.get_barrier_semaphore()
    for k in range(1, n_z):
        pl.semaphore_signal(
            barrier, inc=1, device_id=(tm, (z + k) % n_z * 2 + core), device_id_type=MESH
        )
    for k in range(1, n_tm):
        pl.semaphore_signal(barrier, inc=1, device_id=((tm + k) % n_tm, space), device_id_type=MESH)
    pl.semaphore_signal(barrier, inc=1, device_id=(tm, sibling), device_id_type=MESH)
    for j in range(n_tm):
        wall[j, rows_of(z, hd), :] = wo_ref[:, j * quarter : (j + 1) * quarter]
    xg[space] = x_ref[...]
    kv[0, :, 3 * hd :] = jnp.ones((group, hd), jnp.bfloat16)
    pl.semaphore_wait(barrier, n_z - 1 + n_tm - 1 + 1)

    def norm(value, gain):
        scaled = value * lax.rsqrt(jnp.mean(value * value, axis=-1, keepdims=True) + 1e-06)
        return (scaled * gain).astype(jnp.bfloat16)

    def project(x, weights):
        qkv = jnp.dot(x, weights[...], preferred_element_type=jnp.float32)
        qkv = qkv.astype(jnp.bfloat16)
        query = norm(qkv[:, :hd].astype(jnp.float32), qg_ref[...])
        key = norm(qkv[:, hd : 2 * hd].astype(jnp.float32), kg_ref[...])
        return jnp.concatenate([query, key, qkv[:, 2 * hd :]], axis=1)

    def inside(zz):
        return jnp.logical_and(zz >= 0, zz < n_z)

    def forwards_w(way):
        return z < n_z - 1 if way == 0 else z > 0

    def spread_w(u):
        for way in (0, 1):
            zz = z - u if way == 0 else z + u
            live = inside(zz)

            @pl.when(jnp.logical_and(live, u > 0))
            def _():
                w_ring(way, u - 1, zz).wait_recv()

            @pl.when(jnp.logical_and(live, forwards_w(way)))
            def _():
                w_ring(way, u, zz).start()

            @pl.when(jnp.logical_and(live, u > 0))
            def _():
                for k in range(1, n_tm):
                    w_peer(k, zz, tm).start()

    def step(u, carry):
        def arrive(part):
            for way in (0, 1):
                zz = z - u if way == 0 else z + u

                @pl.when(jnp.logical_and(inside(zz), jnp.logical_and(u > 0, u < n_z - 1)))
                def _():
                    x_ring(way, u - 1, zz, part).wait_recv()

                going = jnp.logical_and(jnp.logical_or(inner, u >= part), u < n_z - 2)

                @pl.when(jnp.logical_and(jnp.logical_and(inside(zz), going), forwards_w(way)))
                def _():
                    x_ring(way, u, zz, part).start()

                live = jnp.logical_and(inside(zz), u < n_z - 1)
                fresh = live if way == 0 else jnp.logical_and(live, u > 0)

                @pl.when(fresh)
                def _():
                    x_sibling(zz, core, part).start()

        arrive(0)

        @pl.when(jnp.logical_and(inner, u == 1))
        def _():
            wq_inward().wait_recv()
            for k in (0, 1):
                wq_peer(k, tm).start()

        arrive(1)

        @pl.when(jnp.logical_and(inner, u == 1))
        def _():
            wq_peer(0, beside).wait_recv()
            wq_peer(2, beside).start()

        last = jnp.logical_and(inner, u == n_z - 2)

        @pl.when(last)
        def _():
            wq_peer(1, across).wait_recv()
            wq_peer(2, (beside + n_tm // 2) % n_tm).wait_recv()
            far = n_z - 1 - end_of

            def send(turn, carry):
                @pl.when(turn == 1)
                def _():
                    for part in (0, 1):
                        x_sibling(far, 1 - core, part).wait_recv()

                slot = far * 2 + core + turn * (1 - 2 * core)
                stage[turn] = project(xg[slot], inner_w)
                qkv_outward(far, turn).start()
                return carry

            lax.fori_loop(0, 2, send, 0)

        @pl.when(outer)
        def _():
            spread_w(u)

        def item(way, carry):
            zz = z - u + way * 2 * u
            fresh = jnp.logical_and(inside(zz), way * (1 - jnp.minimum(u, 1)) == 0)

            @pl.when(jnp.logical_and(fresh, u < n_z - 1))
            def _():
                @pl.when(jnp.logical_not(last))
                def _():
                    for part in (0, 1):
                        x_sibling(zz, 1 - core, part).wait_recv()

                both = xg[rows_of(zz, 2)].reshape(2 * tokens, model)
                kv[0, rows_of(zz, 2 * tokens), 0 : 3 * hd] = project(both, wq_ref)

            for turn in (0, 1):
                side = core + turn * (1 - 2 * core)

                @pl.when(jnp.logical_and(fresh, u == n_z - 1))
                def _():
                    qkv_outward(zz, turn).wait_recv()

                @pl.when(jnp.logical_and(fresh, tm > 0))
                def _():
                    kv_copy(0, zz, side).start()

                @pl.when(jnp.logical_and(fresh, tm < n_tm - 1))
                def _():
                    kv_copy(1, zz, side).start()

            return carry

        lax.fori_loop(0, 2, item, 0)

        for way in (0, 1):

            @pl.when(jnp.logical_and(jnp.logical_and(outer, u == 0), forwards_w(way)))
            def _():
                x_ring(way, u, z, 0).wait_send()
                wq_inward().start()
                wq_inward().wait_send()
                x_ring(way, u, z, 1).start()

        @pl.when(inner)
        def _():
            spread_w(u)

        return carry

    token = perm_ref[...].astype(jnp.float32)
    rows_here, cols, plane = frame

    def whole(value, by):
        return jnp.floor((value + 0.5) * (1.0 / by))

    at_frame = whole(token, plane)
    token = token - at_frame * plane
    row = whole(token, cols)
    col = token - row * cols
    shard = whole(row, rows_here)
    pos = shard * tokens + (at_frame * rows_here + row - shard * rows_here) * cols + col
    for i in range(group // hd):
        block = jnp.broadcast_to(pos[:, i * hd : (i + 1) * hd], (hd, hd))
        place[i * hd : (i + 1) * hd, :] = block.T

    lax.fori_loop(0, n_z, step, 0)

    def others(body):
        for k in range(1, n_z):
            body((z + k) % n_z)

    for way in (0, 1):
        here = 2 - way
        live = tm < n_tm - 1 if way == 0 else tm > 0

        @pl.when(live)
        def _():
            kv[here, :, 3 * hd :] = jnp.ones((group, hd), jnp.bfloat16)

            for zz in range(n_z):
                for side in (0, 1):
                    kv_copy(way, zz, side).wait_recv()

        @pl.when(jnp.logical_not(live))
        def _():
            kv[here, :, hd : 2 * hd] = kv[0, :, hd : 2 * hd]
            kv[here, :, 2 * hd :] = jnp.zeros((group, 2 * hd), jnp.bfloat16)

    factor = math.log2(math.e) * hd**-0.5
    block_rows = 2 * tokens

    def attend_block(i, carry):
        zz = (z + 1 + i) % n_z
        pos = place[rows_of(zz, block_rows), :]
        lanes = lax.broadcasted_iota(jnp.int32, (block_rows, hd), 1).astype(jnp.float32)
        picks = [jnp.where(pos - i * hd == lanes, 1.0, 0.0) for i in range(group // hd)]
        pick = jnp.concatenate([p.astype(jnp.bfloat16) for p in picks], axis=1)
        query = jnp.dot(pick, kv[0, :, 0:hd], preferred_element_type=jnp.float32)
        query = query.astype(jnp.bfloat16)
        highest = None
        for part in range(3):
            score = lax.dot_general(
                query,
                kv[part, :, hd : 2 * hd],
                (((1,), (1,)), ((), ())),
                preferred_element_type=jnp.float32,
            )
            scores[part] = score
            top = jnp.max(score, axis=-1, keepdims=True)
            highest = top if highest is None else jnp.maximum(highest, top)
        total = jnp.zeros((block_rows, 2 * hd), jnp.float32)
        for part in range(3):
            weights = jnp.exp2((scores[part] - highest) * factor).astype(jnp.bfloat16)
            total += jnp.dot(weights, kv[part, :, 2 * hd :], preferred_element_type=jnp.float32)
        result = (total[:, :hd] / total[:, hd:]).astype(jnp.bfloat16)

        @pl.when(zz == z)
        def _():
            attn_in[z] = result

        @pl.when(zz != z)
        def _():
            attn[zz] = result
            attn_copy(zz).start()

        return carry

    lax.fori_loop(0, n_z, attend_block, 0)

    def weights_in(zz):
        for k in range(1, n_tm):
            w_peer(k, zz, (tm + n_tm - k) % n_tm).wait_recv()

    others(weights_in)
    others(lambda zz: attn_arrival(zz).wait_recv())

    def heads(side):
        rows = rows_of(side, tokens)
        return jnp.concatenate([attn_in[zz, rows, :] for zz in range(n_z)], axis=1)

    left = jnp.concatenate([heads(1 - core), heads(core)], axis=0)
    for j in range(n_tm):
        both = jnp.dot(left, wall[j], preferred_element_type=jnp.float32)
        part_out[j] = both[:tokens].astype(jnp.bfloat16)
        part_copy(j).start()
        own[j] = both[tokens:]
    for j in range(n_tm):
        part_copy(j).wait_recv()
        total = own[j] + part_in[j].astype(jnp.float32)
        out_ref[:, j * quarter : (j + 1) * quarter] = total.astype(jnp.bfloat16)

    for j in range(n_tm):
        part_copy(j).wait_send()

    def sent(zz):
        attn_copy(zz).wait_send()
        for k in range(1, n_tm):
            w_peer(k, zz, tm).wait_send()

    others(sent)

    for zz in range(n_z):

        @pl.when(tm > 0)
        def _():
            for side in (0, 1):
                kv_copy(0, zz, side).wait_send()

        @pl.when(tm < n_tm - 1)
        def _():
            for side in (0, 1):
                kv_copy(1, zz, side).wait_send()

        far = jnp.logical_and(outer, zz == n_z - 1 - z)

        @pl.when(jnp.logical_not(far))
        def _():
            for part in (0, 1):
                x_sibling(zz, core, part).wait_send()

    for u in range(n_z - 1):
        for way in (0, 1):
            zz = z - u if way == 0 else z + u

            @pl.when(jnp.logical_and(inside(zz), forwards_w(way)))
            def _():
                w_ring(way, u, zz).wait_send()

            for part in (0, 1):
                live = u < n_z - 2
                if u == 0 and part == 0:
                    live = inner

                @pl.when(jnp.logical_and(jnp.logical_and(live, inside(zz)), forwards_w(way)))
                def _():
                    x_ring(way, u, zz, part).wait_send()

    @pl.when(inner)
    def _():
        wq_peer(0, tm).wait_send()
        wq_peer(1, tm).wait_send()
        wq_peer(2, beside).wait_send()
        for turn in (0, 1):
            qkv_outward(n_z - 1 - end_of, turn).wait_send()


def fused(n_tm, n_z, frame, x, wq, wo, q_gain, k_gain, perm):
    tokens, model = x.shape
    hd = wo.shape[0]
    shards = 2 * n_z
    group = shards * tokens
    bf = jnp.bfloat16
    dma = pltpu.SemaphoreType.DMA
    vmem = pl.BlockSpec(memory_space=pltpu.VMEM)
    return pl.pallas_call(
        functools.partial(fused_kernel, n_tm, n_z, frame),
        out_shape=jax.ShapeDtypeStruct((tokens, model), bf),
        in_specs=[vmem] * 6,
        out_specs=vmem,
        scratch_shapes=[
            pltpu.VMEM((shards, tokens, model), bf),
            pltpu.VMEM((n_tm, n_z * hd, model // n_tm), bf),
            pltpu.VMEM((model, 3 * hd), bf),
            pltpu.VMEM((2, tokens, 3 * hd), bf),
            pltpu.VMEM((group, hd), jnp.float32),
            pltpu.VMEM((3, group, 4 * hd), bf),
            pltpu.VMEM((3, 2 * tokens, group), jnp.float32),
            pltpu.VMEM((n_z, 2 * tokens, hd), bf),
            pltpu.VMEM((n_z, 2 * tokens, hd), bf),
            pltpu.VMEM((n_tm, tokens, model // n_tm), bf),
            pltpu.VMEM((n_tm, tokens, model // n_tm), bf),
            pltpu.VMEM((n_tm, tokens, model // n_tm), jnp.float32),
            dma((2, n_z)),
            dma((2, n_z)),
            dma((n_tm - 1, n_z)),
            dma((n_tm - 1, n_z)),
            dma((2, n_z, 2)),
            dma((2, n_z, 2)),
            dma((n_z, 2)),
            dma((n_z, 2)),
            dma((2, n_z, 2)),
            dma((2, n_z, 2)),
            dma((n_z,)),
            dma((n_z,)),
            dma((n_tm,)),
            dma((n_tm,)),
            dma,
            dma,
            dma((n_tm - 1,)),
            dma((n_tm - 1,)),
            dma((2,)),
            dma((2,)),
        ],
        compiler_params=pltpu.CompilerParams(
            collective_id=0, has_side_effects=True, vmem_limit_bytes=56 * 1024 * 1024
        ),
    )(x, wq, wo, q_gain, k_gain, perm)


def whole_window(video, w_qkv, w_out, q_gain, k_gain, tile_perm):
    frames, rows_here, cols, model = video.shape
    n_tm = lax.axis_size("tm")
    n_space = lax.axis_size("space")
    hd = w_out.shape[1]
    tokens = frames * rows_here * cols
    mixed = fused(
        n_tm,
        n_space // 2,
        (rows_here, cols, rows_here * n_space * cols),
        video.reshape(tokens, model),
        w_qkv.reshape(model, 3 * hd),
        w_out.reshape(hd, model),
        q_gain.reshape(1, hd),
        k_gain.reshape(1, hd),
        tile_perm,
    )
    return mixed[None]


def extended(cells, sides, width):
    for axis, dim in sides:
        count = lax.axis_size(axis)
        ends = count - 1
        head = lax.slice_in_dim(cells, 0, width, axis=dim)
        tail = lax.slice_in_dim(cells, cells.shape[dim] - width, cells.shape[dim], axis=dim)
        cells = jnp.concatenate(
            [
                lax.ppermute(tail, axis, [(i, (i + 1) % count) for i in range(ends)]),
                cells,
                lax.ppermute(head, axis, [((i + 1) % count, i) for i in range(ends)]),
            ],
            axis=dim,
        )
    return cells


def head_norm(values, gain):
    wide = values.astype(jnp.float32)
    scaled = wide * lax.rsqrt(jnp.mean(wide * wide, axis=-1, keepdims=True) + 1e-06)
    return (scaled * gain).astype(jnp.bfloat16)


def attend(queries, chosen, valid):
    heads_here = queries.shape[1]
    head_dim = queries.shape[2]
    span = chosen.shape[1] * chosen.shape[2]
    keys = chosen[:, :, :, :, 0, :].reshape(-1, heads_here, head_dim)
    values = chosen[:, :, :, :, 1, :].reshape(-1, heads_here, head_dim)
    scores = jnp.einsum(
        "qhd,khd->hqk", queries, keys, preferred_element_type=jnp.float32
    ) * head_dim ** (-0.5)
    live = jnp.repeat(valid, span)
    scores = jnp.where(live[None, None, :], scores, -jnp.inf)
    highest = jnp.max(scores, axis=-1, keepdims=True)
    weights = jnp.exp(scores - highest)
    probs = (weights / jnp.sum(weights, axis=-1, keepdims=True)).astype(jnp.bfloat16)
    result = jnp.einsum("hqk,khd->qhd", probs, values, preferred_element_type=jnp.float32)
    return result.astype(jnp.bfloat16)


def per_device(video, w_qkv, w_out, q_gain, k_gain, tile_perm, window):
    tiles = video.shape[0] * video.shape[1] * lax.axis_size("space") * video.shape[2] // (TT * TH * TW)
    sized = lax.axis_size("tm") == 4 and lax.axis_size("space") == 8
    if window.shape[1] == tiles and w_qkv.shape[1] == 1 and sized:
        return whole_window(video, w_qkv, w_out, q_gain, k_gain, tile_perm)
    frames_here = video.shape[0]
    cols_here = video.shape[2]
    model_dim = video.shape[3]
    heads_here = w_qkv.shape[1]
    head_dim = w_out.shape[1]
    flat_w = w_qkv.reshape(model_dim, heads_here * 3 * head_dim)
    qkv = jnp.einsum(
        "frwd,dc->frwc",
        lax.all_gather(video, "space", axis=1, tiled=True),
        flat_w,
        preferred_element_type=jnp.float32,
    ).astype(jnp.bfloat16)
    group_tokens = frames_here * qkv.shape[1] * cols_here
    qkv = qkv.reshape(group_tokens, heads_here, 3, head_dim)
    ordered = jnp.take(qkv, tile_perm[0], axis=0)
    queries = head_norm(ordered[:, :, 0, :], q_gain)
    keys = head_norm(ordered[:, :, 1, :], k_gain)
    pairs = jnp.stack([keys, ordered[:, :, 2, :]], axis=2)
    beside_all = extended(pairs[None], (("tm", 0),), 1)
    tile_tokens = TT * TH * TW
    tile_count = group_tokens // tile_tokens
    beside_all = beside_all.reshape(3, tile_count, tile_tokens, heads_here, 2, head_dim)
    position = lax.axis_index("tm")
    valid = jnp.stack([position > 0, position >= 0, position < lax.axis_size("tm") - 1])
    query_tiles = queries.reshape(tile_count, tile_tokens, heads_here, head_dim)

    def one_tile(item):
        block, picks = item
        return attend(block, jnp.take(beside_all, picks, axis=1), valid)

    attn = lax.map(one_tile, (query_tiles, window)).reshape(group_tokens, heads_here, head_dim)
    flat_attn = attn.reshape(group_tokens, heads_here * head_dim)
    flat_out = w_out.reshape(heads_here * head_dim, model_dim)
    product = jnp.dot(flat_attn, flat_out, preferred_element_type=jnp.float32)
    summed = lax.psum_scatter(
        lax.optimization_barrier(product.astype(jnp.bfloat16))
        .astype(jnp.float32)
        .astype(jnp.bfloat16),
        "space",
        scatter_dimension=0,
        tiled=True,
    )
    return summed[None]


def solution(mesh):
    in_specs = (
        P("tm", "space", None, None),
        P(None, "space", None),
        P("space", None, None),
        P(),
        P(),
        P("tm", None),
        P(),
    )
    out_specs = P("tm", "space", None)
    return jax.shard_map(
        per_device, mesh=mesh, in_specs=in_specs, out_specs=out_specs, check_vma=False
    )
```
